512 devices in a mesh: gx: 16 (over z), gy: 32 (over x, y, core).
Axes of the slice: x: 4, y: 4, z: 16, core: 2. Of those that a mesh axis runs over, the one named last changes fastest.
Arguments:
- defect: float32 [256, 1024, 128], P('gx', 'gy'), may hold values from -6 to 6
- coefficient: float32 [256, 1024, 128], P('gx', 'gy'), may hold values from 0.2 to 2
Outputs:
- correction: float32 [256, 1024, 128], P('gx', 'gy')
The draws below stay inside these ranges and needn't reach their ends.
All inputs are finite; a program needn't handle non-finite values.
Results may differ from the reference program's by a relative error of at most 0.00002.
Values sent between devices are 32-bit elements; how exact they have to be, the bound alone decides.
A program may use at most 64 MiB of HBM per device.

```python
import math
import jax
import jax.numpy as jnp

LEVELS = 7
SWEEPS = 2
COARSE_SWEEPS = 8
NX = 256
NY = 1024
NZ = 128


def draw_defect(key, part):
    key = jax.random.fold_in(key, 11)
    shape = (NX, NY, NZ)
    return jax.random.truncated_normal(key, -6.0, 6.0, shape, jnp.float32)


def levels(key, shape, split, low, top_value):
    level, own = 1.0, jax.random.fold_in(key, 6)
    for position, shards_of in split:
        heights = jnp.exp(jax.random.uniform(jax.random.fold_in(own, position), (shards_of,), jnp.float32, low / len(split), top_value / len(split)))
        level = level * jnp.repeat(heights, shape[position] // shards_of).reshape([-1 if axis == position else 1 for axis in range(len(shape))])
    return level


def setup_inputs(seed: int = 0) -> dict:
    key_list = jax.random.split(jax.random.key(seed), 3)
    return {
        "defect": draw_defect(jax.random.fold_in(key_list[2], 71), 0),
        "coefficient": jnp.clip(jnp.exp(math.log(2.0) - 2.3025851 * jax.random.uniform(key_list[1], (NX, NY, NZ), jnp.float32) ** levels(key_list[1], (NX, NY, NZ), ((0, 16), (1, 32)), -0.2, 0.2)), 0.2, 2.0),
    }


damping = 0.7
directions = ((1, 0, 0), (-1, 0, 0), (0, 1, 0), (0, -1, 0), (0, 0, 1), (0, 0, -1))


def neighbour(padded, offset):
    extent = padded.shape
    return padded[1 + offset[0]:extent[0] - 1 + offset[0], 1 + offset[1]:extent[1] - 1 + offset[1], 1 + offset[2]:extent[2] - 1 + offset[2]]


def stencil(padded, coefficient, factor):
    extended = jnp.pad(padded, ((0, 0), (0, 0), (1, 1)))
    conduct = jnp.pad(coefficient, ((0, 0), (0, 0), (1, 1)))
    centre = neighbour(extended, (0, 0, 0))
    centre_coeff = neighbour(conduct, (0, 0, 0))
    fluxes = jnp.zeros_like(centre)
    weights = jnp.zeros_like(centre)
    for offset in directions:
        face = (0.5 * factor) * (centre_coeff + neighbour(conduct, offset))
        fluxes = fluxes + face * (centre - neighbour(extended, offset))
        weights = weights + face
    return fluxes, weights


def coarsen(values):
    summed = values[0::2] + values[1::2]
    summed = summed[:, 0::2] + summed[:, 1::2]
    summed = summed[:, :, 0::2] + summed[:, :, 1::2]
    return 0.125 * summed


def prolong(values):
    return jnp.repeat(jnp.repeat(jnp.repeat(values, 2, 0), 2, 1), 2, 2)


def pad_sides(values):
    return jnp.pad(values, ((1, 1), (1, 1), (0, 0)))


def jacobi_whole(iterate, source, padded_coeff, factor):
    applied, diagonal = stencil(pad_sides(iterate), padded_coeff, factor)
    return iterate + damping * (source - applied) / diagonal


def whole_cycle(source, coefficient, degree):
    factor = 0.25 ** degree
    padded_coeff = pad_sides(coefficient)
    iterate = jnp.zeros_like(source)
    if degree == LEVELS - 1:
        for sweep_no in range(COARSE_SWEEPS):
            iterate = jacobi_whole(iterate, source, padded_coeff, factor)
        return iterate
    for sweep_no in range(SWEEPS):
        iterate = jacobi_whole(iterate, source, padded_coeff, factor)
    applied = stencil(pad_sides(iterate), padded_coeff, factor)[0]
    coarse = whole_cycle(coarsen(source - applied), coarsen(coefficient), degree + 1)
    iterate = iterate + prolong(coarse)
    for sweep_no in range(SWEEPS):
        iterate = jacobi_whole(iterate, source, padded_coeff, factor)
    return iterate


def reference(defect, coefficient):
    return whole_cycle(defect, coefficient, 0)
```

```python
import functools

import jax
import jax.numpy as jnp
from jax import lax
from jax.experimental import pallas as pl
from jax.experimental.pallas import tpu as pltpu
from jax.sharding import PartitionSpec as P

MESH = pl.DeviceIdType.MESH
DAMP = 0.7
KEEP = 0.3
COARSE_SWEEPS = 8
LANES = 128
f32 = jnp.float32

BX, BY = (16, 8, 4), (32, 16, 8)
HX, HY = (4, 8, 4), (4, 8, 4)
EX = tuple(b + 2 * h for b, h in zip(BX, HX))
EY = tuple(b + 2 * h for b, h in zip(BY, HY))

NEAR = [(a, b) for a in (-1, 0, 1) for b in (-1, 0, 1) if (a, b) != (0, 0)]


def ahead(t, d):
    return pltpu.roll(t, (-d) % LANES, axis=t.ndim - 1)


def rows_ahead(t, d):
    n = t.shape[-2]
    return pltpu.roll(t, (-d) % n, axis=t.ndim - 2)


def planes_ahead(t, d):
    d = d % t.shape[0]
    return jnp.concatenate([t[d:], t[:d]], axis=0) if d else t


def lane_iota(shape):
    return lax.broadcasted_iota(jnp.int32, shape, len(shape) - 1)


def bit(lane, b):
    return (lane & (1 << b)) != 0


def swap(t, b):
    on = bit(lane_iota(t.shape), b)
    return jnp.where(on, ahead(t, -(1 << b)), ahead(t, 1 << b))


def spread(t, b, value):
    on = bit(lane_iota(t.shape), b)
    if value:
        return jnp.where(on, t, ahead(t, 1 << b))
    return jnp.where(on, ahead(t, -(1 << b)), t)


def loop(lo, hi, body, unroll=1):
    def step(i, c):
        body(i)
        return c

    lax.fori_loop(lo, hi, step, 0, unroll=unroll)


class Block:
    def __init__(self, level, gx, gy, nx, ny, refs):
        self.level = level
        self.factor = 0.25**level
        self.zs = 1 << level
        self.bx, self.by, self.hx, self.hy = BX[level], BY[level], HX[level], HY[level]
        self.ex, self.ey = EX[level], EY[level]
        self.gx, self.gy, self.nx, self.ny = gx, gy, nx, ny
        self.k, self.s, self.va, self.vb, self.wx, self.wy, self.wz, self.inv, self.dg = refs
        shape = (self.ey, LANES)
        self.lane = lane_iota(shape)
        y = gy * self.by - self.hy + lax.broadcasted_iota(jnp.int32, shape, 0)
        self.row_in = jnp.where((y >= 0) & (y < ny * self.by), 1.0, 0.0).astype(f32)

    def inside(self, x):
        gx = self.gx * self.bx - self.hx + x
        return self.row_in * jnp.where((gx >= 0) & (gx < self.nx * self.bx), 1.0, 0.0).astype(f32)

    def weights(self, lo, hi, unroll=1):
        half = 0.5 * self.factor
        last = self.lane >= LANES - self.zs
        first = self.lane < self.zs

        def step(x, carry):
            kc, fxm = carry
            m = self.inside(x)
            kn = self.k[x + 1] * self.inside(x + 1)
            fxp = half * (kc + kn)
            fyp = half * (kc + rows_ahead(kc, 1))
            fzp = half * (kc + jnp.where(last, 0.0, ahead(kc, self.zs)))
            wz = jnp.where(last, 0.0, fzp)
            fzm = jnp.where(first, half * kc, ahead(wz, -self.zs))
            diag = ((fxm + fxp) + (rows_ahead(fyp, -1) + fyp)) + (fzp + fzm)
            self.wx[x] = fxp
            self.wy[x] = fyp
            self.wz[x] = wz
            self.dg[x] = diag
            self.inv[x] = jnp.where(m > 0, DAMP / diag, 0.0)
            return kn, fxp

        k0 = self.k[lo - 1] * self.inside(lo - 1)
        k1 = self.k[lo] * self.inside(lo)
        self.wx[lo - 1] = half * (k0 + k1)
        lax.fori_loop(lo, hi, step, (k1, half * (k0 + k1)), unroll=unroll)

    def first(self, src, dst, lo, hi, unroll=1):
        def step(x):
            dst[x] = self.inv[x] * src[x]

        loop(lo, hi, step, unroll)

    def pull(self, v, x):
        c = v[x]
        wy, wz = self.wy[x], self.wz[x]
        t = self.wx[x] * v[x + 1] + self.wx[x - 1] * v[x - 1]
        u = wy * rows_ahead(c, 1) + rows_ahead(wy * c, -1)
        w = wz * ahead(c, self.zs) + ahead(wz * c, -self.zs)
        return c, (t + u) + w

    def sweep(self, s, src, dst, lo, hi, unroll=1, shift=0):
        def step(x):
            c, near = self.pull(src, x)
            dst[x - shift] = KEEP * c + self.inv[x] * (s[x] + near)

        loop(lo, hi, step, unroll)

    def residual(self, s, v, x):
        c, near = self.pull(v, x)
        return (s[x] - self.dg[x] * c) + near

    def restrict(self, plane, tmp, lo, pairs, row, count, put, unroll=1):
        lane = lane_iota((count, LANES))

        def step(i):
            x = lo + 2 * i
            t = plane(x) + plane(x + 1)
            tmp[i, pl.ds(0, t.shape[0]), :] = t
            t = tmp[i, pl.ds(row, count, stride=2), :] + tmp[i, pl.ds(row + 1, count, stride=2), :]
            put(i, 0.125 * (t + swap(t, self.level)))

        loop(0, pairs, step, unroll)

    def slabs(self, ref, wx, wy):
        parts = []
        for dx, dy in NEAR:
            spans = []
            for d, h, b, w in ((dx, self.hx, self.bx, wx), (dy, self.hy, self.by, wy)):
                if d == 0:
                    spans.append((h, h, b))
                elif d > 0:
                    spans.append((h + b - w, h - w, w))
                else:
                    spans.append((h, h + b, w))
            (sx, tx, cx), (sy, ty, cy) = spans
            parts.append(
                (
                    ref.at[pl.ds(sx, cx), pl.ds(sy, cy), :],
                    ref.at[pl.ds(tx, cx), pl.ds(ty, cy), :],
                )
            )
        return parts


class Whole:
    def __init__(self, factor, k, near, masks, inside):
        half = 0.5 * factor
        self.near = near
        diag = None
        self.w = []
        for n, mask in zip(near(k), masks):
            face = half * (k + n)
            self.w.append(jnp.where(mask, face, 0.0))
            face = jnp.where(mask, face, half * k)
            diag = face if diag is None else diag + face
        self.diag = diag
        inv = DAMP / diag
        self.inv = inv if inside is None else jnp.where(inside, inv, 0.0)

    def pull(self, v):
        total = None
        for n, w in zip(self.near(v), self.w):
            total = w * n if total is None else total + w * n
        return total

    def sweep(self, s, v):
        return KEEP * v + self.inv * (s + self.pull(v))

    def residual(self, s, v):
        return (s - self.diag * v) + self.pull(v)


def kernel(nx, ny, *refs):
    s_in, k_in, out = refs[:3]
    level_refs = [refs[3 + 9 * l : 12 + 9 * l] for l in range(3)]
    (
        tmp, rep, sv2, pack, acc, halo3, v3s, bcc, own4, v4s,
        local_sem, s0_sems, r0_sems, s1_sems, r1_sems, s2_sems, r2_sems,
        sa_sem, ra_sem, sh_sems, rh_sems, sb_sem, rb_sem,
    ) = refs[30:]
    gx, gy = lax.axis_index("gx"), lax.axis_index("gy")
    gh = nx // 8

    def there(dx, dy):
        return (lax.rem(gx + dx + nx, nx), lax.rem(gy + dy + ny, ny))

    L = [Block(l, gx, gy, nx, ny, level_refs[l]) for l in range(3)]
    l0, l1, l2 = L
    own0 = (pl.ds(HX[0], BX[0]), pl.ds(HY[0], BY[0]))
    loads = [
        pltpu.make_async_copy(k_in, l0.k.at[own0[0], own0[1], :], local_sem.at[0]),
        pltpu.make_async_copy(s_in, l0.s.at[own0[0], own0[1], :], local_sem.at[1]),
    ]
    for c in loads:
        c.start()

    column = [(i, j) for i in range(nx) for j in (-1, 0, 1) if (i, j) != (0, 0)]
    line = [(0, j) for j in range(1, ny)]
    column.sort(key=lambda o: -min(o[0], nx - o[0]))
    peers = column + [(0, j) for j in range(2, ny - 1)]
    acc[...] = jnp.zeros_like(acc)
    v3s[...] = jnp.zeros_like(v3s)
    barrier = pltpu.get_barrier_semaphore()
    for dx, dy in peers:
        pl.semaphore_signal(barrier, inc=1, device_id=there(dx, dy), device_id_type=MESH)
    for c in loads:
        c.wait()

    def put_k1(i, t):
        l1.k[HX[1] + i, pl.ds(HY[1], BY[1]), :] = t

    l0.restrict(lambda x: l0.k[x, own0[1], :], tmp, HX[0], BX[1], 0, BY[1], put_k1)

    pl.semaphore_wait(barrier, len(peers))

    pending = []

    def send(parts, ssems, rsems, base=0):
        copies = []
        for i, (dx, dy) in enumerate(NEAR):
            src, dst = parts[i]
            c = pltpu.make_async_remote_copy(
                src, dst, ssems.at[base + i], rsems.at[base + i], device_id=there(dx, dy), device_id_type=MESH
            )
            c.start()
            copies.append(c)
        pending.extend(copies)
        return copies

    got_k0 = send(l0.slabs(l0.k, 4, 4), s0_sems, r0_sems, 0)
    got_s0 = send(l0.slabs(l0.s, 3, 3), s0_sems, r0_sems, 8)
    got_k1 = send(l1.slabs(l1.k, 8, 8), s1_sems, r1_sems, 0)

    for c in got_k0:
        c.wait_recv()
    l0.weights(1, EX[0] - 1)
    for c in got_s0:
        c.wait_recv()
    l0.first(l0.s, l0.va, 1, EX[0] - 1)
    l0.sweep(l0.s, l0.va, l0.vb, 2, EX[0] - 2)

    def put_s1(i, t):
        l1.s[HX[1] + i, pl.ds(HY[1], BY[1]), :] = t

    l0.restrict(lambda x: l0.residual(l0.s, l0.vb, x), tmp, HX[0], BX[1], HY[0], BY[1], put_s1)
    got_s1 = send(l1.slabs(l1.s, 6, 8), s1_sems, r1_sems, 8)

    for c in got_k1:
        c.wait_recv()

    def put_k2(i, t):
        l2.k[i] = t

    l1.restrict(lambda x: l1.k[x], tmp, 0, EX[2], 0, EY[2], put_k2)
    l1.weights(1, EX[1] - 1)
    l2.weights(1, EX[2] - 1)

    def packed(plane_ref):
        t = plane_ref[...]
        lane = lane_iota(t.shape)
        sub = lax.broadcasted_iota(jnp.int32, t.shape, 0)
        return jnp.sum(jnp.where((lane & 7) == sub, t, 0.0), axis=0, keepdims=True)

    def put_pack(i, t):
        pack[pl.ds(4 * i, 4), :] = t

    l2.restrict(lambda x: l2.k[x], tmp, HX[2], 2, HY[2], 4, put_pack, unroll=True)
    acc[1, gx, pl.ds(1, 1), :] = packed(pack)

    for c in got_s1:
        c.wait_recv()
    l1.first(l1.s, l1.va, 2, EX[1] - 2)
    l1.sweep(l1.s, l1.va, l1.vb, 3, EX[1] - 3)

    def put_s2(i, t):
        l2.s[2 + i] = t

    l1.restrict(lambda x: l1.residual(l1.s, l1.vb, x), tmp, 4, 8, 0, EY[2], put_s2)

    l2.first(l2.s, l2.va, 2, EX[2] - 2, unroll=True)
    l2.sweep(l2.s, l2.va, l2.vb, 3, EX[2] - 3, unroll=True)
    l2.restrict(lambda x: l2.residual(l2.s, l2.vb, x), tmp, HX[2], 2, HY[2], 4, put_pack, unroll=True)
    acc[0, gx, pl.ds(1, 1), :] = packed(pack)

    got_a = []
    for n, (dx, dy) in enumerate(column):
        c = pltpu.make_async_remote_copy(
            acc.at[:, gx, pl.ds(1, 1), :],
            acc.at[:, gx, pl.ds(1 - dy, 1), :],
            sa_sem.at[n],
            ra_sem.at[n],
            device_id=there(dx, dy),
            device_id_type=MESH,
        )
        c.start()
        got_a.append(c)

    own2 = (pl.ds(HX[2], BX[2]), pl.ds(HY[2], BY[2]))
    sv2[0, own2[0], own2[1], :] = l2.s[own2[0], own2[1], :]
    sv2[1, own2[0], own2[1], :] = l2.vb[own2[0], own2[1], :]
    got_sv = send(l2.slabs(sv2.at[0], 4, 4), s2_sems, r2_sems, 0)
    got_sv += send(l2.slabs(sv2.at[1], 4, 4), s2_sems, r2_sems, 8)

    for c in got_a:
        c.wait_recv()

    shape = (nx, 8, LANES)
    lane = lane_iota(shape)
    px = lax.broadcasted_iota(jnp.int32, shape, 0)
    py = gy - 1 + lax.broadcasted_iota(jnp.int32, shape, 1)
    b2, yl, z3 = bit(lane, 2), lane & 3, lane >> 3

    def near3(v):
        up, down = ahead(v, 4), ahead(v, -4)
        return (
            jnp.where(b2, planes_ahead(down, 1), up),
            jnp.where(b2, down, planes_ahead(up, -1)),
            jnp.where(yl == 3, rows_ahead(ahead(v, -3), 1), ahead(v, 1)),
            jnp.where(yl == 0, rows_ahead(ahead(v, 3), -1), ahead(v, -1)),
            ahead(v, 8),
            ahead(v, -8),
        )

    x3, y3 = 2 * px + jnp.where(b2, 1, 0), 4 * py + yl
    in3 = (py >= 0) & (py < ny) & (py < gy + 2)
    w3 = Whole(
        0.25**3,
        jnp.where(in3, acc[1], 0.0),
        near3,
        (x3 < 2 * nx - 1, x3 > 0, y3 < 4 * ny - 1, y3 > 0, z3 < 15, z3 > 0),
        in3,
    )
    s3 = acc[0]
    v = w3.inv * s3
    v = w3.sweep(s3, v)
    v3s[pl.ds(1, nx)] = v
    r3 = w3.residual(s3, v)

    def coarse4(t):
        t = t + swap(t, 2)
        t = t + swap(t, 0)
        t = 0.125 * (t + swap(t, 3))
        on0, on2, on3 = (bit(lane_iota((8, LANES)), b) for b in (0, 2, 3))
        rows = []
        for h in range(gh):
            p = [t[8 * h + i] for i in range(8)]
            p = [jnp.where(on0, p[2 * i + 1], p[2 * i]) for i in range(4)]
            p = [jnp.where(on2, p[2 * i + 1], p[2 * i]) for i in range(2)]
            rows.append(jnp.where(on3, p[1], p[0])[1:2])
        return rows

    mine = jnp.concatenate(coarse4(r3) + coarse4(acc[1]), axis=0)
    own4[pl.ds(0, 2 * gh), :] = mine
    bcc[pl.ds(pl.multiple_of(8 * gy, 8), 2 * gh), :] = mine
    got_b = []
    for n, (dx, dy) in enumerate(line):
        c = pltpu.make_async_remote_copy(
            own4.at[pl.ds(0, 2 * gh), :],
            bcc.at[pl.ds(pl.multiple_of(8 * gy, 8), 2 * gh), :],
            sb_sem.at[n],
            rb_sem.at[n],
            device_id=there(dx, dy),
            device_id_type=MESH,
        )
        c.start()
        got_b.append(c)
    got_h = []
    for n, dy in enumerate((1, -1)):
        c = pltpu.make_async_remote_copy(
            v3s.at[pl.ds(1, nx), pl.ds(1, 1), :],
            halo3.at[:, pl.ds(1 - dy, 1), :],
            sh_sems.at[n],
            rh_sems.at[n],
            device_id=there(0, dy),
            device_id_type=MESH,
        )
        c.start()
        got_h.append(c)
    for c in got_b:
        c.wait_recv()

    s4 = jnp.stack([bcc[pl.ds(h, ny, stride=8), :] for h in range(gh)])
    k4 = jnp.stack([bcc[pl.ds(gh + h, ny, stride=8), :] for h in range(gh)])
    shape = (gh, ny, LANES)
    lane = lane_iota(shape)
    top = lax.broadcasted_iota(jnp.int32, shape, 0)
    py = lax.broadcasted_iota(jnp.int32, shape, 1)
    b0, b1, low = bit(lane, 0), bit(lane, 1), lane & 13

    def near4(v):
        up, down = ahead(v, 2), ahead(v, -2)
        return (
            jnp.where(low == 13, planes_ahead(ahead(v, -13), 1), jnp.where(b0, ahead(v, 3), ahead(v, 1))),
            jnp.where(low == 0, planes_ahead(ahead(v, 13), -1), jnp.where(b0, ahead(v, -1), ahead(v, -3))),
            jnp.where(b1, rows_ahead(down, 1), up),
            jnp.where(b1, down, rows_ahead(up, -1)),
            ahead(v, 16),
            ahead(v, -16),
        )

    y4, z4 = 2 * py + jnp.where(b1, 1, 0), lane >> 4
    w4 = Whole(
        0.25**4,
        k4,
        near4,
        (
            (low < 13) | (top < gh - 1),
            (low > 0) | (top > 0),
            y4 < 2 * ny - 1,
            y4 > 0,
            z4 < 7,
            z4 > 0,
        ),
        None,
    )

    def coarse5(t):
        t = t + swap(t, 0)
        t = t + swap(t, 1)
        t = 0.125 * (t + swap(t, 4))
        if gh == 1:
            return t[0]
        return jnp.where(bit(lane_iota((ny, LANES)), 0), t[1], t[0])

    shape = (ny, LANES)
    lane = lane_iota(shape)
    row = lax.broadcasted_iota(jnp.int32, shape, 0)
    mid, z5, z6 = lane & 12, lane >> 5, lane >> 6
    c0, c3 = bit(lane, 0), bit(lane, 3)
    end_hi = c0 if gh == 2 else lane >= 0
    end_lo = ~c0 if gh == 2 else lane >= 0

    def near5(v):
        return (
            jnp.where(mid == 12, ahead(v, -11), ahead(v, 4)),
            jnp.where(mid == 0, ahead(v, 11), ahead(v, -4)),
            rows_ahead(v, 1),
            rows_ahead(v, -1),
            ahead(v, 32),
            ahead(v, -32),
        )

    def near6(v):
        return (
            jnp.where(c3, ahead(v, -7), ahead(v, 8)),
            jnp.where(c3, ahead(v, -8), ahead(v, 7)),
            rows_ahead(v, 2),
            rows_ahead(v, -2),
            ahead(v, 64),
            ahead(v, -64),
        )

    k5 = coarse5(k4)
    w5 = Whole(
        0.25**5,
        k5,
        near5,
        (~((mid == 12) & end_hi), ~((mid == 0) & end_lo), row < ny - 1, row > 0, z5 < 3, z5 > 0),
        None,
    )

    def coarse6(t):
        t = t + swap(t, 2)
        t = t + swap(t, 5)
        odd = (row & 1) != 0
        return 0.125 * (t + jnp.where(odd, rows_ahead(t, -1), rows_ahead(t, 1)))

    w6 = Whole(
        0.25**6,
        coarse6(k5),
        near6,
        (~(c3 & end_hi), ~((~c3) & end_lo), row < ny - 2, row > 1, z6 < 1, z6 > 0),
        None,
    )

    v4 = w4.inv * s4
    v4 = w4.sweep(s4, v4)
    s5 = coarse5(w4.residual(s4, v4))
    v5 = w5.inv * s5
    v5 = w5.sweep(s5, v5)
    s6 = coarse6(w5.residual(s5, v5))
    v6 = w6.inv * s6
    v6 = lax.fori_loop(0, COARSE_SWEEPS - 1, lambda i, t: w6.sweep(s6, t), v6)
    v5 = v5 + v6
    v5 = w5.sweep(s5, v5)
    v5 = w5.sweep(s5, v5)
    if gh == 1:
        v4 = v4 + v5[None]
    else:
        v4 = v4 + jnp.stack([spread(v5, 0, 0), spread(v5, 0, 1)])
    v4 = w4.sweep(s4, v4)
    v4 = w4.sweep(s4, v4)
    v4s[:, pl.ds(8, ny), :] = v4

    for c in got_h:
        c.wait_recv()
    planes = []
    for h in range(gh):
        t = [v4s[h, pl.ds(7 + gy, 8), :]]
        for b in (3, 2, 0):
            t = [spread(q, b, value) for q in t for value in (0, 1)]
        planes += t
    sub = lax.broadcasted_iota(jnp.int32, (nx, 8, LANES), 1)
    v = jnp.where(sub == 1, v3s[pl.ds(1, nx)], halo3[...]) + jnp.stack(planes)
    v = jnp.where(in3, v, 0.0)
    v = w3.sweep(s3, v)
    v = w3.sweep(s3, v)
    for c in got_h:
        c.wait_send()
    v3s[pl.ds(1, nx)] = v

    for c in got_sv:
        c.wait_recv()
    shape = (8, LANES)
    lane, sub = lane_iota(shape), lax.broadcasted_iota(jnp.int32, shape, 0)
    for d in range(3):
        t = v3s[gx + d]
        rows = [jnp.broadcast_to(t[i : i + 1], shape) for i in range(3)]
        rows = jnp.where(sub < 2, rows[0], jnp.where(sub < 6, rows[1], rows[2]))
        for xl in range(2):
            t = jnp.where((lane & 7) == 4 * xl + ((sub + 2) & 3), rows, 0.0)
            for b in range(3):
                t = t + swap(t, b)
            n = 2 * d + xl
            rep[n, pl.ds(0, 8, stride=2), :] = t
            rep[n, pl.ds(1, 8, stride=2), :] = t
            t = rep[n, pl.ds(0, EY[2]), :]
            for e in range(2):
                x = 2 * n + e
                l2.va[x] = jnp.where(l2.inside(x) > 0, sv2[1, x] + t, 0.0)
    l2.sweep(sv2.at[0], l2.va, l2.vb, 1, EX[2] - 1, unroll=True)
    l2.sweep(sv2.at[0], l2.vb, l2.va, 2, EX[2] - 2, unroll=True)

    def up1(i):
        t = l2.va[i + 2]
        rep[i, pl.ds(0, EY[2], stride=2), :] = t
        rep[i, pl.ds(1, EY[2], stride=2), :] = t
        t = rep[i, pl.ds(0, EY[1]), :]
        for e in range(2):
            x = 2 * i + 4 + e
            l1.va[x] = l1.vb[x] + t

    loop(0, 8, up1)
    l1.sweep(l1.s, l1.va, l1.vb, 6, EX[1] - 6)
    l1.sweep(l1.s, l1.vb, l1.va, 7, EX[1] - 7)

    def up0(i):
        t = l1.va[i + 7]
        rep[i, pl.ds(4, EY[1], stride=2), :] = t
        rep[i, pl.ds(5, EY[1], stride=2), :] = t
        t = rep[i, pl.ds(16, EY[0]), :]
        for e in range(2):
            x = 2 * i + 2 + e
            l0.va[x] = l0.vb[x] + t

    loop(0, 10, up0)
    l0.sweep(l0.s, l0.va, l0.vb, 3, EX[0] - 3)
    l0.sweep(l0.s, l0.vb, l0.va, 4, EX[0] - 4)
    c = pltpu.make_async_copy(l0.va.at[own0[0], own0[1], :], out, local_sem.at[0])
    c.start()
    for p in pending + got_a + got_b:
        p.wait_send()
    c.wait()


def solution(mesh):
    nx, ny = mesh.shape["gx"], mesh.shape["gy"]

    def body(defect, coefficient):
        dma = pltpu.SemaphoreType.DMA
        scratch = []
        for l in range(3):
            scratch += [pltpu.VMEM((EX[l], EY[l], LANES), f32)] * 9
        scratch += [
            pltpu.VMEM((12, EY[0], LANES), f32),
            pltpu.VMEM((12, 72, LANES), f32),
            pltpu.VMEM((2, EX[2], EY[2], LANES), f32),
            pltpu.VMEM((8, LANES), f32),
            pltpu.VMEM((2, nx, 8, LANES), f32),
            pltpu.VMEM((nx, 8, LANES), f32),
            pltpu.VMEM((nx + 2, 8, LANES), f32),
            pltpu.VMEM((8 * ny, LANES), f32),
            pltpu.VMEM((8, LANES), f32),
            pltpu.VMEM((nx // 8, ny + 16, LANES), f32),
            dma((2,)),
            dma((16,)), dma((16,)), dma((16,)), dma((16,)), dma((16,)), dma((16,)),
            dma((3 * nx - 1,)), dma((3 * nx - 1,)), dma((2,)), dma((2,)), dma((ny - 1,)), dma((ny - 1,)),
        ]
        return pl.pallas_call(
            functools.partial(kernel, nx, ny),
            out_shape=jax.ShapeDtypeStruct(defect.shape, f32),
            in_specs=[pl.BlockSpec(memory_space=pl.ANY)] * 2,
            out_specs=pl.BlockSpec(memory_space=pl.ANY),
            scratch_shapes=scratch,
            compiler_params=pltpu.CompilerParams(
                collective_id=0, has_side_effects=True, vmem_limit_bytes=40 << 20
            ),
        )(defect, coefficient)

    placed = P("gx", "gy", None)
    return jax.shard_map(
        body, mesh=mesh, in_specs=(placed, placed), out_specs=placed, check_vma=False
    )
```

```python
import functools

import jax
import jax.numpy as jnp
from jax import lax
from jax.experimental import pallas as pl
from jax.experimental.pallas import tpu as pltpu
from jax.sharding import PartitionSpec as P

MESH = pl.DeviceIdType.MESH
DAMP = 0.7
KEEP = 0.3
COARSE_SWEEPS = 8
LANES = 128
f32 = jnp.float32
U0W, U0S, U0R, U1W, U1S, U1R, U2W = 11, 10, 4, 11, 9, 4, 99

BX, BY = (16, 8, 4), (32, 16, 8)
HX, HY = (4, 8, 4), (4, 8, 4)
EX = tuple(b + 2 * h for b, h in zip(BX, HX))
EY = tuple(b + 2 * h for b, h in zip(BY, HY))

NEAR = [(a, b) for a in (-1, 0, 1) for b in (-1, 0, 1) if (a, b) != (0, 0)]


def ahead(t, d):
    return pltpu.roll(t, (-d) % LANES, axis=t.ndim - 1)


def rows_ahead(t, d):
    n = t.shape[-2]
    return pltpu.roll(t, (-d) % n, axis=t.ndim - 2)


def planes_ahead(t, d):
    d = d % t.shape[0]
    return jnp.concatenate([t[d:], t[:d]], axis=0) if d else t


def lane_iota(shape):
    return lax.broadcasted_iota(jnp.int32, shape, len(shape) - 1)


def bit(lane, b):
    return (lane & (1 << b)) != 0


def swap(t, b):
    on = bit(lane_iota(t.shape), b)
    return jnp.where(on, ahead(t, -(1 << b)), ahead(t, 1 << b))


def spread(t, b, value):
    on = bit(lane_iota(t.shape), b)
    if value:
        return jnp.where(on, t, ahead(t, 1 << b))
    return jnp.where(on, ahead(t, -(1 << b)), t)


def loop(lo, hi, body, unroll=1, carry=()):
    rounds = (hi - lo) // unroll

    def step(r, c):
        for j in range(unroll):
            c = body(lo + unroll * r + j, c)
        return c

    if rounds > 1:
        carry = lax.fori_loop(0, rounds, step, carry)
    else:
        rounds = 0
    for i in range(lo + unroll * rounds, hi):
        carry = body(i, carry)
    return carry


K0, S0, K1, S1, GA, SV, GB, H3 = range(8)


def phase_rows(nx, ny):
    def rim(level, wx, wy):
        bx, by = BX[level], BY[level]
        return (bx + 2 * wx) * (by + 2 * wy) - bx * by

    return (
        rim(0, 4, 4),
        rim(0, 3, 3),
        rim(1, 8, 8),
        rim(1, 6, 8),
        2 * (3 * nx - 1),
        2 * rim(2, 4, 4),
        (ny - 1) * 2 * (nx // 8),
        2 * nx,
    )


class Block:
    def __init__(self, level, gx, gy, nx, ny, refs):
        self.level = level
        self.factor = 0.25**level
        self.zs = 1 << level
        self.bx, self.by, self.hx, self.hy = BX[level], BY[level], HX[level], HY[level]
        self.ex, self.ey = EX[level], EY[level]
        self.gx, self.gy, self.nx, self.ny = gx, gy, nx, ny
        self.k, self.s, self.va, self.vb, self.wx, self.wy, self.wz, self.inv, self.dg = refs
        shape = (self.ey, LANES)
        self.lane = lane_iota(shape)
        y = gy * self.by - self.hy + lax.broadcasted_iota(jnp.int32, shape, 0)
        self.row_in = jnp.where((y >= 0) & (y < ny * self.by), 1.0, 0.0).astype(f32)

    def inside(self, x):
        gx = self.gx * self.bx - self.hx + x
        return self.row_in * jnp.where((gx >= 0) & (gx < self.nx * self.bx), 1.0, 0.0).astype(f32)

    def weights(self, lo, hi, unroll=1):
        half = 0.5 * self.factor
        last = self.lane >= LANES - self.zs
        first = self.lane < self.zs

        def step(x, carry):
            kc, fxm = carry
            m = self.inside(x)
            kn = self.k[x + 1] * self.inside(x + 1)
            fxp = half * (kc + kn)
            fyp = half * (kc + rows_ahead(kc, 1))
            fzp = half * (kc + jnp.where(last, 0.0, ahead(kc, self.zs)))
            wz = jnp.where(last, 0.0, fzp)
            fzm = jnp.where(first, half * kc, ahead(wz, -self.zs))
            diag = ((fxm + fxp) + (rows_ahead(fyp, -1) + fyp)) + (fzp + fzm)
            self.wx[x] = fxp
            self.wy[x] = fyp
            self.wz[x] = wz
            self.dg[x] = diag
            self.inv[x] = jnp.where(m > 0, DAMP / diag, 0.0)
            return kn, fxp

        k0 = self.k[lo - 1] * self.inside(lo - 1)
        k1 = self.k[lo] * self.inside(lo)
        self.wx[lo - 1] = half * (k0 + k1)
        loop(lo, hi, step, unroll, (k1, half * (k0 + k1)))

    def first(self, src, dst, lo, hi, unroll=1):
        def step(x, c):
            dst[x] = self.inv[x] * src[x]
            return c

        loop(lo, hi, step, unroll)

    def pull(self, v, x):
        c = v[x]
        wy, wz = self.wy[x], self.wz[x]
        t = self.wx[x] * v[x + 1] + self.wx[x - 1] * v[x - 1]
        u = wy * rows_ahead(c, 1) + rows_ahead(wy * c, -1)
        w = wz * ahead(c, self.zs) + ahead(wz * c, -self.zs)
        return c, (t + u) + w

    def sweep(self, s, src, dst, lo, hi, unroll=1, shift=0):
        def step(x, carry):
            c, near = self.pull(src, x)
            dst[x - shift] = KEEP * c + self.inv[x] * (s[x] + near)
            return carry

        loop(lo, hi, step, unroll)

    def residual(self, s, v, x):
        c, near = self.pull(v, x)
        return (s[x] - self.dg[x] * c) + near

    def restrict(self, plane, tmp, lo, pairs, row, count, put, unroll=1):
        lane = lane_iota((count, LANES))

        def step(i, c):
            x = lo + 2 * i
            t = plane(x) + plane(x + 1)
            tmp[i, pl.ds(0, t.shape[0]), :] = t
            t = tmp[i, pl.ds(row, count, stride=2), :] + tmp[i, pl.ds(row + 1, count, stride=2), :]
            put(i, 0.125 * (t + swap(t, self.level)))
            return c

        loop(0, pairs, step, unroll)

    def slabs(self, ref, wx, wy):
        parts = []
        for dx, dy in NEAR:
            spans = []
            for d, h, b, w in ((dx, self.hx, self.bx, wx), (dy, self.hy, self.by, wy)):
                if d == 0:
                    spans.append((h, h, b))
                elif d > 0:
                    spans.append((h + b - w, h - w, w))
                else:
                    spans.append((h, h + b, w))
            (sx, tx, cx), (sy, ty, cy) = spans
            parts.append(
                (
                    ref.at[pl.ds(sx, cx), pl.ds(sy, cy), :],
                    ref.at[pl.ds(tx, cx), pl.ds(ty, cy), :],
                )
            )
        return parts


class Whole:
    def __init__(self, factor, k, near, masks, inside):
        half = 0.5 * factor
        self.near = near
        diag = None
        self.w = []
        for n, mask in zip(near(k), masks):
            face = half * (k + n)
            self.w.append(jnp.where(mask, face, 0.0))
            face = jnp.where(mask, face, half * k)
            diag = face if diag is None else diag + face
        self.diag = diag
        inv = DAMP / diag
        self.inv = inv if inside is None else jnp.where(inside, inv, 0.0)

    def pull(self, v):
        total = None
        for n, w in zip(self.near(v), self.w):
            total = w * n if total is None else total + w * n
        return total

    def sweep(self, s, v):
        return KEEP * v + self.inv * (s + self.pull(v))

    def residual(self, s, v):
        return (s - self.diag * v) + self.pull(v)


def kernel(nx, ny, *refs):
    s_in, k_in, out = refs[:3]
    level_refs = [refs[3 + 9 * l : 12 + 9 * l] for l in range(3)]
    (
        tmp, rep, sv2, pack, acc, halo3, v3s, v3u, bcc, own4, v4s, ruler,
        local_sem, out_sem, ssem, rsem, known,
    ) = refs[30:]
    gx, gy = lax.axis_index("gx"), lax.axis_index("gy")
    gh = nx // 8
    ROWS = phase_rows(nx, ny)

    def there(dx, dy):
        return (lax.rem(gx + dx + nx, nx), lax.rem(gy + dy + ny, ny))

    L = [Block(l, gx, gy, nx, ny, level_refs[l]) for l in range(3)]
    l0, l1, l2 = L
    own0 = (pl.ds(HX[0], BX[0]), pl.ds(HY[0], BY[0]))
    loads = [
        pltpu.make_async_copy(k_in, l0.k.at[own0[0], own0[1], :], local_sem.at[0]),
        pltpu.make_async_copy(s_in, l0.s.at[own0[0], own0[1], :], local_sem.at[1]),
    ]
    for c in loads:
        c.start()

    column = [(i, j) for i in range(nx) for j in (-1, 0, 1) if (i, j) != (0, 0)]
    line = [(0, j) for j in range(1, ny)]
    column.sort(key=lambda o: -min(o[0], nx - o[0]))
    acc[...] = jnp.zeros_like(acc)
    v3u[...] = jnp.zeros_like(v3u)
    barrier = pltpu.get_barrier_semaphore()
    for dx, dy in NEAR:
        pl.semaphore_signal(barrier, inc=1, device_id=there(dx, dy), device_id_type=MESH)
    for c in loads:
        c.wait()

    pl.semaphore_wait(barrier, len(NEAR))

    def remote(src, dst, phase, dx, dy):
        c = pltpu.make_async_remote_copy(
            src, dst, ssem.at[phase], rsem.at[phase], device_id=there(dx, dy), device_id_type=MESH
        )
        c.start()

    def tell(step):
        d = 1 << step
        targets = [(0, d), (0, -d)]
        if d <= nx // 4:
            targets += [(d, 0), (-d, 0)]
        for dx, dy in targets:
            pl.semaphore_signal(known.at[step], inc=1, device_id=there(dx, dy), device_id_type=MESH)

    def told(step):
        pl.semaphore_wait(known.at[step], 4 if (1 << step) <= nx // 4 else 2)

    def all_of(phase):
        part = ruler.at[pl.ds(0, ROWS[phase]), :]
        return pltpu.make_async_remote_copy(
            part, part, ssem.at[phase], rsem.at[phase], device_id=there(1, 0), device_id_type=MESH
        )

    def received(phase):
        all_of(phase).wait_recv()

    def send(parts, phase):
        for (dx, dy), (src, dst) in zip(NEAR, parts):
            remote(src, dst, phase, dx, dy)

    tell(0)
    send(l0.slabs(l0.k, 4, 4), K0)
    send(l0.slabs(l0.s, 3, 3), S0)

    def put_k1(i, t):
        l1.k[HX[1] + i, pl.ds(HY[1], BY[1]), :] = t

    l0.restrict(lambda x: l0.k[x, own0[1], :], tmp, HX[0], BX[1], 0, BY[1], put_k1, U0R)
    send(l1.slabs(l1.k, 8, 8), K1)
    told(0)
    tell(1)

    received(K0)
    l0.weights(1, EX[0] - 1, U0W)
    received(S0)
    l0.first(l0.s, l0.va, 1, EX[0] - 1, U0W)
    l0.sweep(l0.s, l0.va, l0.vb, 2, EX[0] - 2, U0S)

    def put_s1(i, t):
        l1.s[HX[1] + i, pl.ds(HY[1], BY[1]), :] = t

    l0.restrict(lambda x: l0.residual(l0.s, l0.vb, x), tmp, HX[0], BX[1], HY[0], BY[1], put_s1, U0R)
    send(l1.slabs(l1.s, 6, 8), S1)
    told(1)
    tell(2)

    received(K1)

    def put_k2(i, t):
        l2.k[i] = t

    l1.restrict(lambda x: l1.k[x], tmp, 0, EX[2], 0, EY[2], put_k2, 6)
    l1.weights(1, EX[1] - 1, U1W)
    l2.weights(1, EX[2] - 1, U2W)

    def packed(plane_ref):
        t = plane_ref[...]
        lane = lane_iota(t.shape)
        sub = lax.broadcasted_iota(jnp.int32, t.shape, 0)
        return jnp.sum(jnp.where((lane & 7) == sub, t, 0.0), axis=0, keepdims=True)

    def put_pack(i, t):
        pack[pl.ds(4 * i, 4), :] = t

    l2.restrict(lambda x: l2.k[x], tmp, HX[2], 2, HY[2], 4, put_pack, unroll=99)
    acc[1, gx, pl.ds(1, 1), :] = packed(pack)

    received(S1)
    told(2)
    tell(3)
    l1.first(l1.s, l1.va, 2, EX[1] - 2, 10)
    l1.sweep(l1.s, l1.va, l1.vb, 3, EX[1] - 3, U1S)

    def put_s2(i, t):
        l2.s[2 + i] = t

    l1.restrict(lambda x: l1.residual(l1.s, l1.vb, x), tmp, 4, 8, 0, EY[2], put_s2, U1R)

    l2.first(l2.s, l2.va, 2, EX[2] - 2, unroll=99)
    l2.sweep(l2.s, l2.va, l2.vb, 3, EX[2] - 3, unroll=99)
    l2.restrict(lambda x: l2.residual(l2.s, l2.vb, x), tmp, HX[2], 2, HY[2], 4, put_pack, unroll=99)
    acc[0, gx, pl.ds(1, 1), :] = packed(pack)

    for dx, dy in column:
        remote(acc.at[:, gx, pl.ds(1, 1), :], acc.at[:, gx, pl.ds(1 - dy, 1), :], GA, dx, dy)

    own2 = (pl.ds(HX[2], BX[2]), pl.ds(HY[2], BY[2]))
    sv2[0, own2[0], own2[1], :] = l2.s[own2[0], own2[1], :]
    sv2[1, own2[0], own2[1], :] = l2.vb[own2[0], own2[1], :]
    for q in range(2):
        send(l2.slabs(sv2.at[q], 4, 4), SV)

    received(GA)

    shape = (nx, 8, LANES)
    lane = lane_iota(shape)
    px = lax.broadcasted_iota(jnp.int32, shape, 0)
    py = gy - 1 + lax.broadcasted_iota(jnp.int32, shape, 1)
    b2, yl, z3 = bit(lane, 2), lane & 3, lane >> 3

    def near3(v):
        up, down = ahead(v, 4), ahead(v, -4)
        return (
            jnp.where(b2, planes_ahead(down, 1), up),
            jnp.where(b2, down, planes_ahead(up, -1)),
            jnp.where(yl == 3, rows_ahead(ahead(v, -3), 1), ahead(v, 1)),
            jnp.where(yl == 0, rows_ahead(ahead(v, 3), -1), ahead(v, -1)),
            ahead(v, 8),
            ahead(v, -8),
        )

    x3, y3 = 2 * px + jnp.where(b2, 1, 0), 4 * py + yl
    in3 = (py >= 0) & (py < ny) & (py < gy + 2)
    w3 = Whole(
        0.25**3,
        jnp.where(in3, acc[1], 0.0),
        near3,
        (x3 < 2 * nx - 1, x3 > 0, y3 < 4 * ny - 1, y3 > 0, z3 < 15, z3 > 0),
        in3,
    )
    s3 = acc[0]
    v = w3.inv * s3
    v = w3.sweep(s3, v)
    v3s[...] = v
    r3 = w3.residual(s3, v)

    def coarse4(t):
        t = t + swap(t, 2)
        t = t + swap(t, 0)
        t = 0.125 * (t + swap(t, 3))
        on0, on2, on3 = (bit(lane_iota((8, LANES)), b) for b in (0, 2, 3))
        rows = []
        for h in range(gh):
            p = [t[8 * h + i] for i in range(8)]
            p = [jnp.where(on0, p[2 * i + 1], p[2 * i]) for i in range(4)]
            p = [jnp.where(on2, p[2 * i + 1], p[2 * i]) for i in range(2)]
            rows.append(jnp.where(on3, p[1], p[0])[1:2])
        return rows

    mine = jnp.concatenate(coarse4(r3) + coarse4(acc[1]), axis=0)
    own4[pl.ds(0, 2 * gh), :] = mine
    bcc[pl.ds(pl.multiple_of(8 * gy, 8), 2 * gh), :] = mine
    told(3)
    for dx, dy in line:
        remote(
            own4.at[pl.ds(0, 2 * gh), :],
            bcc.at[pl.ds(pl.multiple_of(8 * gy, 8), 2 * gh), :],
            GB,
            dx,
            dy,
        )
    for dy in (1, -1):
        remote(v3s.at[:, pl.ds(1, 1), :], halo3.at[:, pl.ds(1 - dy, 1), :], H3, 0, dy)
    received(GB)

    s4 = jnp.stack([bcc[pl.ds(h, ny, stride=8), :] for h in range(gh)])
    k4 = jnp.stack([bcc[pl.ds(gh + h, ny, stride=8), :] for h in range(gh)])
    shape = (gh, ny, LANES)
    lane = lane_iota(shape)
    top = lax.broadcasted_iota(jnp.int32, shape, 0)
    py = lax.broadcasted_iota(jnp.int32, shape, 1)
    b0, b1, low = bit(lane, 0), bit(lane, 1), lane & 13

    def near4(v):
        up, down = ahead(v, 2), ahead(v, -2)
        return (
            jnp.where(low == 13, planes_ahead(ahead(v, -13), 1), jnp.where(b0, ahead(v, 3), ahead(v, 1))),
            jnp.where(low == 0, planes_ahead(ahead(v, 13), -1), jnp.where(b0, ahead(v, -1), ahead(v, -3))),
            jnp.where(b1, rows_ahead(down, 1), up),
            jnp.where(b1, down, rows_ahead(up, -1)),
            ahead(v, 16),
            ahead(v, -16),
        )

    y4, z4 = 2 * py + jnp.where(b1, 1, 0), lane >> 4
    w4 = Whole(
        0.25**4,
        k4,
        near4,
        (
            (low < 13) | (top < gh - 1),
            (low > 0) | (top > 0),
            y4 < 2 * ny - 1,
            y4 > 0,
            z4 < 7,
            z4 > 0,
        ),
        None,
    )

    def coarse5(t):
        t = t + swap(t, 0)
        t = t + swap(t, 1)
        t = 0.125 * (t + swap(t, 4))
        if gh == 1:
            return t[0]
        return jnp.where(bit(lane_iota((ny, LANES)), 0), t[1], t[0])

    shape = (ny, LANES)
    lane = lane_iota(shape)
    row = lax.broadcasted_iota(jnp.int32, shape, 0)
    mid, z5, z6 = lane & 12, lane >> 5, lane >> 6
    c0, c3 = bit(lane, 0), bit(lane, 3)
    end_hi = c0 if gh == 2 else lane >= 0
    end_lo = ~c0 if gh == 2 else lane >= 0

    def near5(v):
        return (
            jnp.where(mid == 12, ahead(v, -11), ahead(v, 4)),
            jnp.where(mid == 0, ahead(v, 11), ahead(v, -4)),
            rows_ahead(v, 1),
            rows_ahead(v, -1),
            ahead(v, 32),
            ahead(v, -32),
        )

    def near6(v):
        return (
            jnp.where(c3, ahead(v, -7), ahead(v, 8)),
            jnp.where(c3, ahead(v, -8), ahead(v, 7)),
            rows_ahead(v, 2),
            rows_ahead(v, -2),
            ahead(v, 64),
            ahead(v, -64),
        )

    k5 = coarse5(k4)
    w5 = Whole(
        0.25**5,
        k5,
        near5,
        (~((mid == 12) & end_hi), ~((mid == 0) & end_lo), row < ny - 1, row > 0, z5 < 3, z5 > 0),
        None,
    )

    def coarse6(t):
        t = t + swap(t, 2)
        t = t + swap(t, 5)
        odd = (row & 1) != 0
        return 0.125 * (t + jnp.where(odd, rows_ahead(t, -1), rows_ahead(t, 1)))

    w6 = Whole(
        0.25**6,
        coarse6(k5),
        near6,
        (~(c3 & end_hi), ~((~c3) & end_lo), row < ny - 2, row > 1, z6 < 1, z6 > 0),
        None,
    )

    v4 = w4.inv * s4
    v4 = w4.sweep(s4, v4)
    s5 = coarse5(w4.residual(s4, v4))
    v5 = w5.inv * s5
    v5 = w5.sweep(s5, v5)
    s6 = coarse6(w5.residual(s5, v5))
    v6 = w6.inv * s6
    v6 = lax.fori_loop(0, COARSE_SWEEPS - 1, lambda i, t: w6.sweep(s6, t), v6)
    v5 = v5 + v6
    v5 = w5.sweep(s5, v5)
    v5 = w5.sweep(s5, v5)
    if gh == 1:
        v4 = v4 + v5[None]
    else:
        v4 = v4 + jnp.stack([spread(v5, 0, 0), spread(v5, 0, 1)])
    v4 = w4.sweep(s4, v4)
    v4 = w4.sweep(s4, v4)
    v4s[:, pl.ds(8, ny), :] = v4

    received(H3)
    planes = []
    for h in range(gh):
        t = [v4s[h, pl.ds(7 + gy, 8), :]]
        for b in (3, 2, 0):
            t = [spread(q, b, value) for q in t for value in (0, 1)]
        planes += t
    sub = lax.broadcasted_iota(jnp.int32, (nx, 8, LANES), 1)
    v = jnp.where(sub == 1, v3s[...], halo3[...]) + jnp.stack(planes)
    v = jnp.where(in3, v, 0.0)
    v = w3.sweep(s3, v)
    v = w3.sweep(s3, v)
    v3u[pl.ds(1, nx)] = v

    received(SV)
    shape = (8, LANES)
    lane, sub = lane_iota(shape), lax.broadcasted_iota(jnp.int32, shape, 0)
    for d in range(3):
        t = v3u[gx + d]
        rows = [jnp.broadcast_to(t[i : i + 1], shape) for i in range(3)]
        rows = jnp.where(sub < 2, rows[0], jnp.where(sub < 6, rows[1], rows[2]))
        for xl in range(2):
            t = jnp.where((lane & 7) == 4 * xl + ((sub + 2) & 3), rows, 0.0)
            for b in range(3):
                t = t + swap(t, b)
            n = 2 * d + xl
            rep[n, pl.ds(0, 8, stride=2), :] = t
            rep[n, pl.ds(1, 8, stride=2), :] = t
            t = rep[n, pl.ds(0, EY[2]), :]
            for e in range(2):
                x = 2 * n + e
                l2.va[x] = jnp.where(l2.inside(x) > 0, sv2[1, x] + t, 0.0)
    l2.sweep(sv2.at[0], l2.va, l2.vb, 1, EX[2] - 1, unroll=99)
    l2.sweep(sv2.at[0], l2.vb, l2.va, 2, EX[2] - 2, unroll=99)

    def up1(i, c):
        t = l2.va[i + 2]
        rep[i, pl.ds(0, EY[2], stride=2), :] = t
        rep[i, pl.ds(1, EY[2], stride=2), :] = t
        t = rep[i, pl.ds(0, EY[1]), :]
        for e in range(2):
            x = 2 * i + 4 + e
            l1.va[x] = l1.vb[x] + t
        return c

    loop(0, 8, up1, 4)
    l1.sweep(l1.s, l1.va, l1.vb, 6, EX[1] - 6, 6)
    l1.sweep(l1.s, l1.vb, l1.va, 7, EX[1] - 7, 5)

    def up0(i, c):
        t = l1.va[i + 7]
        rep[i, pl.ds(4, EY[1], stride=2), :] = t
        rep[i, pl.ds(5, EY[1], stride=2), :] = t
        t = rep[i, pl.ds(16, EY[0]), :]
        for e in range(2):
            x = 2 * i + 2 + e
            l0.va[x] = l0.vb[x] + t
        return c

    loop(0, 10, up0, 5)
    l0.sweep(l0.s, l0.va, l0.vb, 3, EX[0] - 3, 9)
    chunk = BX[0] // 4
    copies = []
    for i in range(4):
        lo = HX[0] + chunk * i
        l0.sweep(l0.s, l0.vb, l0.va, lo, lo + chunk, chunk)
        c = pltpu.make_async_copy(
            l0.va.at[pl.ds(lo, chunk), own0[1], :], out.at[pl.ds(chunk * i, chunk)], out_sem.at[i]
        )
        c.start()
        copies.append(c)
    for phase in range(len(ROWS)):
        all_of(phase).wait_send()
    for c in copies:
        c.wait()


def solution(mesh):
    nx, ny = mesh.shape["gx"], mesh.shape["gy"]

    def body(defect, coefficient):
        dma = pltpu.SemaphoreType.DMA
        rows = phase_rows(nx, ny)
        scratch = []
        for l in range(3):
            scratch += [pltpu.VMEM((EX[l], EY[l], LANES), f32)] * 9
        scratch += [
            pltpu.VMEM((12, EY[0], LANES), f32),
            pltpu.VMEM((12, 72, LANES), f32),
            pltpu.VMEM((2, EX[2], EY[2], LANES), f32),
            pltpu.VMEM((8, LANES), f32),
            pltpu.VMEM((2, nx, 8, LANES), f32),
            pltpu.VMEM((nx, 8, LANES), f32),
            pltpu.VMEM((nx, 8, LANES), f32),
            pltpu.VMEM((nx + 2, 8, LANES), f32),
            pltpu.VMEM((8 * ny, LANES), f32),
            pltpu.VMEM((8, LANES), f32),
            pltpu.VMEM((nx // 8, ny + 16, LANES), f32),
            pltpu.VMEM((max(rows), LANES), f32),
            dma((2,)),
            dma((4,)),
            dma((len(rows),)),
            dma((len(rows),)),
            pltpu.SemaphoreType.REGULAR((4,)),
        ]
        return pl.pallas_call(
            functools.partial(kernel, nx, ny),
            out_shape=jax.ShapeDtypeStruct(defect.shape, f32),
            in_specs=[pl.BlockSpec(memory_space=pltpu.HBM)] * 2,
            out_specs=pl.BlockSpec(memory_space=pl.ANY),
            scratch_shapes=scratch,
            compiler_params=pltpu.CompilerParams(
                collective_id=0, has_side_effects=True, vmem_limit_bytes=54784 << 10
            ),
        )(defect, coefficient)

    placed = P("gx", "gy", None)
    return jax.shard_map(
        body, mesh=mesh, in_specs=(placed, placed), out_specs=placed, check_vma=False
    )
```

```python
import functools

import jax
import jax.numpy as jnp
from jax import lax
from jax.experimental import pallas as pl
from jax.experimental.pallas import tpu as pltpu
from jax.sharding import PartitionSpec as P

MESH = pl.DeviceIdType.MESH
DAMP = 0.7
KEEP = 0.3
COARSE_SWEEPS = 8
LANES = 128
f32 = jnp.float32
U0W, U0S, U0R, U1W, U1S, U1R, U2W = 10, 9, 4, 11, 9, 4, 99

BX, BY = (16, 8, 4), (32, 16, 8)
HX, HY = (4, 8, 4), (4, 8, 4)
EX = tuple(b + 2 * h for b, h in zip(BX, HX))
EY = tuple(b + 2 * h for b, h in zip(BY, HY))

NEAR = [(1, 1), (1, -1), (-1, 1), (-1, -1), (1, 0), (-1, 0), (0, 1), (0, -1)]


def ahead(t, d):
    return pltpu.roll(t, (-d) % LANES, axis=t.ndim - 1)


def rows_ahead(t, d):
    n = t.shape[-2]
    return pltpu.roll(t, (-d) % n, axis=t.ndim - 2)


def planes_ahead(t, d):
    d = d % t.shape[0]
    return jnp.concatenate([t[d:], t[:d]], axis=0) if d else t


def lane_iota(shape):
    return lax.broadcasted_iota(jnp.int32, shape, len(shape) - 1)


def bit(lane, b):
    return (lane & (1 << b)) != 0


def swap(t, b):
    on = bit(lane_iota(t.shape), b)
    return jnp.where(on, ahead(t, -(1 << b)), ahead(t, 1 << b))


def spread(t, b, value):
    on = bit(lane_iota(t.shape), b)
    if value:
        return jnp.where(on, t, ahead(t, 1 << b))
    return jnp.where(on, ahead(t, -(1 << b)), t)


def loop(lo, hi, body, unroll=1, carry=()):
    rounds = (hi - lo) // unroll

    def step(r, c):
        for j in range(unroll):
            c = body(lo + unroll * r + j, c)
        return c

    if rounds > 1:
        carry = lax.fori_loop(0, rounds, step, carry)
    else:
        rounds = 0
    for i in range(lo + unroll * rounds, hi):
        carry = body(i, carry)
    return carry


K0, S0, K1, S1, GA, SV, GB, H3, V0 = range(9)


def phase_rows(nx, ny):
    def rim(level, wx, wy):
        bx, by = BX[level], BY[level]
        return (bx + 2 * wx) * (by + 2 * wy) - bx * by

    return (
        rim(0, 3, 3),
        rim(0, 2, 2),
        rim(1, 8, 8),
        rim(1, 6, 6),
        2 * (3 * nx - 1),
        2 * rim(2, 4, 4),
        4 * (ny - 1),
        2 * nx,
        rim(0, 2, 2),
    )


class Block:
    def __init__(self, level, gx, gy, nx, ny, refs):
        self.level = level
        self.factor = 0.25**level
        self.zs = 1 << level
        self.bx, self.by, self.hx, self.hy = BX[level], BY[level], HX[level], HY[level]
        self.ex, self.ey = EX[level], EY[level]
        self.gx, self.gy, self.nx, self.ny = gx, gy, nx, ny
        self.k, self.s, self.va, self.vb, self.wx, self.wy, self.wz, self.inv, self.dg = refs
        shape = (self.ey, LANES)
        self.lane = lane_iota(shape)
        y = gy * self.by - self.hy + lax.broadcasted_iota(jnp.int32, shape, 0)
        self.row_in = jnp.where((y >= 0) & (y < ny * self.by), 1.0, 0.0).astype(f32)

    def inside(self, x):
        gx = self.gx * self.bx - self.hx + x
        return self.row_in * jnp.where((gx >= 0) & (gx < self.nx * self.bx), 1.0, 0.0).astype(f32)

    def weights(self, lo, hi, unroll=1):
        half = 0.5 * self.factor
        last = self.lane >= LANES - self.zs
        first = self.lane < self.zs

        def step(x, carry):
            kc, fxm = carry
            m = self.inside(x)
            kn = self.k[x + 1] * self.inside(x + 1)
            fxp = half * (kc + kn)
            fyp = half * (kc + rows_ahead(kc, 1))
            fzp = half * (kc + jnp.where(last, 0.0, ahead(kc, self.zs)))
            wz = jnp.where(last, 0.0, fzp)
            fzm = jnp.where(first, half * kc, ahead(wz, -self.zs))
            diag = ((fxm + fxp) + (rows_ahead(fyp, -1) + fyp)) + (fzp + fzm)
            self.wx[x] = fxp
            self.wy[x] = fyp
            self.wz[x] = wz
            self.dg[x] = diag
            self.inv[x] = jnp.where(m > 0, DAMP / diag, 0.0)
            return kn, fxp

        k0 = self.k[lo - 1] * self.inside(lo - 1)
        k1 = self.k[lo] * self.inside(lo)
        self.wx[lo - 1] = half * (k0 + k1)
        loop(lo, hi, step, unroll, (k1, half * (k0 + k1)))

    def first(self, src, dst, lo, hi, unroll=1):
        def step(x, c):
            dst[x] = self.inv[x] * src[x]
            return c

        loop(lo, hi, step, unroll)

    def pull(self, v, x):
        c = v[x]
        wy, wz = self.wy[x], self.wz[x]
        t = self.wx[x] * v[x + 1] + self.wx[x - 1] * v[x - 1]
        u = wy * rows_ahead(c, 1) + rows_ahead(wy * c, -1)
        w = wz * ahead(c, self.zs) + ahead(wz * c, -self.zs)
        return c, (t + u) + w

    def sweep(self, s, src, dst, lo, hi, unroll=1, shift=0):
        def step(x, carry):
            c, near = self.pull(src, x)
            dst[x - shift] = KEEP * c + self.inv[x] * (s[x] + near)
            return carry

        loop(lo, hi, step, unroll)

    def residual(self, s, v, x):
        c, near = self.pull(v, x)
        return (s[x] - self.dg[x] * c) + near

    def restrict(self, plane, tmp, lo, pairs, row, count, put, unroll=1):
        lane = lane_iota((count, LANES))

        def step(i, c):
            x = lo + 2 * i
            t = plane(x) + plane(x + 1)
            tmp[i, pl.ds(0, t.shape[0]), :] = t
            t = tmp[i, pl.ds(row, count, stride=2), :] + tmp[i, pl.ds(row + 1, count, stride=2), :]
            put(i, 0.125 * (t + swap(t, self.level)))
            return c

        loop(0, pairs, step, unroll)

    def slabs(self, ref, wx, wy):
        parts = []
        for dx, dy in NEAR:
            spans = []
            for d, h, b, w in ((dx, self.hx, self.bx, wx), (dy, self.hy, self.by, wy)):
                if d == 0:
                    spans.append((h, h, b))
                elif d > 0:
                    spans.append((h + b - w, h - w, w))
                else:
                    spans.append((h, h + b, w))
            (sx, tx, cx), (sy, ty, cy) = spans
            parts.append(
                (
                    ref.at[pl.ds(sx, cx), pl.ds(sy, cy), :],
                    ref.at[pl.ds(tx, cx), pl.ds(ty, cy), :],
                )
            )
        return parts


class Whole:
    def __init__(self, factor, k, near, masks, inside=None):
        half = 0.5 * factor
        self.near = near
        faces, parts = [], []
        for n, mask in zip(near(k), masks):
            face = half * (k + n)
            faces.append(jnp.where(mask, face, 0.0))
            parts.append(jnp.where(mask, face, half * k))
        diag = (parts[0] + parts[1]) + (parts[2] + parts[3]) + (parts[4] + parts[5])
        inv = DAMP / diag
        self.inv = inv if inside is None else jnp.where(inside, inv, 0.0)
        self.w = [face * self.inv for face in faces]
        self.back = diag * (1.0 / DAMP)

    def pull(self, v):
        t = [w * n for w, n in zip(self.w, self.near(v))]
        return (t[0] + t[1]) + (t[2] + t[3]) + (t[4] + t[5])

    def sweep(self, q, v):
        return (KEEP * v + q) + self.pull(v)

    def residual(self, q, v):
        return ((q - DAMP * v) + self.pull(v)) * self.back


def kernel(nx, ny, *refs):
    s_in, k_in, out = refs[:3]
    level_refs = [refs[3 + 9 * l : 12 + 9 * l] for l in range(3)]
    (
        tmp, rep, sv2, vh, pack, acc, halo3, v3s, v3u, bcc, own4, v4s, ruler,
        local_sem, out_sem, ssem, rsem, known,
    ) = refs[30:]
    gx, gy = lax.axis_index("gx"), lax.axis_index("gy")
    ROWS = phase_rows(nx, ny)

    def there(dx, dy):
        return (lax.rem(gx + dx + nx, nx), lax.rem(gy + dy + ny, ny))

    L = [Block(l, gx, gy, nx, ny, level_refs[l]) for l in range(3)]
    l0, l1, l2 = L
    own0 = (pl.ds(HX[0], BX[0]), pl.ds(HY[0], BY[0]))
    loads = [
        pltpu.make_async_copy(k_in, l0.k.at[own0[0], own0[1], :], local_sem.at[0]),
        pltpu.make_async_copy(s_in, l0.s.at[own0[0], own0[1], :], local_sem.at[1]),
    ]
    for c in loads:
        c.start()

    column = [(i, j) for i in range(nx) for j in (-1, 0, 1) if (i, j) != (0, 0)]
    line = [(0, j) for j in range(1, ny)]
    line.sort(key=lambda o: -sum(min(c % 4, -c % 4) for c in (o[1] // 2, o[1] // 8)))
    column.sort(key=lambda o: -min(o[0], nx - o[0]))
    v3u[...] = jnp.zeros_like(v3u)
    barrier = pltpu.get_barrier_semaphore()
    for dx, dy in NEAR:
        pl.semaphore_signal(barrier, inc=1, device_id=there(dx, dy), device_id_type=MESH)
    for c in loads:
        c.wait()

    pl.semaphore_wait(barrier, len(NEAR))

    def remote(src, dst, phase, dx, dy):
        c = pltpu.make_async_remote_copy(
            src, dst, ssem.at[phase], rsem.at[phase], device_id=there(dx, dy), device_id_type=MESH
        )
        c.start()

    def tell(step):
        d = 1 << step
        targets = [(0, d), (0, -d)]
        if d <= nx // 4:
            targets += [(d, 0), (-d, 0)]
        for dx, dy in targets:
            pl.semaphore_signal(known.at[step], inc=1, device_id=there(dx, dy), device_id_type=MESH)

    def told(step):
        pl.semaphore_wait(known.at[step], 4 if (1 << step) <= nx // 4 else 2)

    def all_of(phase):
        part = ruler.at[pl.ds(0, ROWS[phase]), :]
        return pltpu.make_async_remote_copy(
            part, part, ssem.at[phase], rsem.at[phase], device_id=there(1, 0), device_id_type=MESH
        )

    def received(phase):
        all_of(phase).wait_recv()

    def send(parts, phase):
        for (dx, dy), (src, dst) in zip(NEAR, parts):
            remote(src, dst, phase, dx, dy)

    tell(0)
    send(l0.slabs(l0.k, 3, 3), K0)
    send(l0.slabs(l0.s, 2, 2), S0)

    def put_k1(i, t):
        l1.k[HX[1] + i, pl.ds(HY[1], BY[1]), :] = t

    l0.restrict(lambda x: l0.k[x, own0[1], :], tmp, HX[0], BX[1], 0, BY[1], put_k1, U0R)
    send(l1.slabs(l1.k, 8, 8), K1)
    told(0)
    tell(1)

    received(K0)
    l0.weights(2, EX[0] - 2, U0W)
    received(S0)
    l0.first(l0.s, l0.va, 2, EX[0] - 2, U0W)
    l0.sweep(l0.s, l0.va, l0.vb, 3, EX[0] - 3, U0S)

    def put_s1(i, t):
        l1.s[HX[1] + i, pl.ds(HY[1], BY[1]), :] = t

    l0.restrict(lambda x: l0.residual(l0.s, l0.vb, x), tmp, HX[0], BX[1], HY[0], BY[1], put_s1, U0R)
    send(l1.slabs(l1.s, 6, 6), S1)
    told(1)
    tell(2)
    for (dx, dy), (src, _), (_, dst) in zip(NEAR, l0.slabs(l0.vb, 2, 2), l0.slabs(vh, 2, 2)):
        remote(src, dst, V0, dx, dy)

    received(K1)

    def put_k2(i, t):
        l2.k[i] = t

    l1.restrict(lambda x: l1.k[x], tmp, 0, EX[2], 0, EY[2], put_k2, 6)
    l1.weights(1, EX[1] - 1, U1W)
    l2.weights(1, EX[2] - 1, U2W)

    def packed(plane_ref):
        t = plane_ref[...]
        lane = lane_iota(t.shape)
        sub = lax.broadcasted_iota(jnp.int32, t.shape, 0)
        return jnp.sum(jnp.where((lane & 7) == sub, t, 0.0), axis=0, keepdims=True)

    def put_pack(i, t):
        pack[pl.ds(4 * i, 4), :] = t

    l2.restrict(lambda x: l2.k[x], tmp, HX[2], 2, HY[2], 4, put_pack, unroll=99)
    acc[1, 1, pl.ds(gx, 1), :] = packed(pack)

    received(S1)
    told(2)
    tell(3)
    l1.first(l1.s, l1.va, 2, EX[1] - 2, 10)
    l1.sweep(l1.s, l1.va, l1.vb, 3, EX[1] - 3, U1S)

    def put_s2(i, t):
        l2.s[2 + i] = t

    l1.restrict(lambda x: l1.residual(l1.s, l1.vb, x), tmp, 4, 8, 0, EY[2], put_s2, U1R)

    l2.first(l2.s, l2.va, 2, EX[2] - 2, unroll=99)
    l2.sweep(l2.s, l2.va, l2.vb, 3, EX[2] - 3, unroll=99)
    l2.restrict(lambda x: l2.residual(l2.s, l2.vb, x), tmp, HX[2], 2, HY[2], 4, put_pack, unroll=99)
    acc[0, 1, pl.ds(gx, 1), :] = packed(pack)

    for dx, dy in column:
        remote(acc.at[:, 1, pl.ds(gx, 1), :], acc.at[:, 1 - dy, pl.ds(gx, 1), :], GA, dx, dy)

    received(GA)

    shape = (3, nx, LANES)
    lane = lane_iota(shape)
    px = lax.broadcasted_iota(jnp.int32, shape, 1)
    py = gy - 1 + lax.broadcasted_iota(jnp.int32, shape, 0)
    b2, yl, z3 = bit(lane, 2), lane & 3, lane >> 3

    def near3(v):
        up, down = ahead(v, 4), ahead(v, -4)
        return (
            jnp.where(b2, rows_ahead(down, 1), up),
            jnp.where(b2, down, rows_ahead(up, -1)),
            jnp.where(yl == 3, planes_ahead(ahead(v, -3), 1), ahead(v, 1)),
            jnp.where(yl == 0, planes_ahead(ahead(v, 3), -1), ahead(v, -1)),
            ahead(v, 8),
            ahead(v, -8),
        )

    x3, y3 = 2 * px + jnp.where(b2, 1, 0), 4 * py + yl
    in3 = (py >= 0) & (py < ny)
    w3 = Whole(
        0.25**3,
        jnp.where(in3, acc[1], 0.0),
        near3,
        (x3 < 2 * nx - 1, x3 > 0, y3 < 4 * ny - 1, y3 > 0, z3 < 15, z3 > 0),
        in3,
    )
    q3 = w3.inv * acc[0]
    v = w3.sweep(q3, q3)
    v3s[...] = v[1]
    r3 = w3.residual(q3, v)[1]

    shape = (nx, LANES)
    lane, sub = lane_iota(shape), lax.broadcasted_iota(jnp.int32, shape, 0)
    place = ((lane >> 1) & 6) + (lane & 1) == (sub >> 1)
    odd = (sub & 1) != 0

    def coarse4(t):
        t = t + swap(t, 2)
        t = t + swap(t, 0)
        t = 0.125 * (t + swap(t, 3))
        t = jnp.where(place, t, 0.0)
        return [jnp.sum(jnp.where(odd == h, t, 0.0), axis=0, keepdims=True) for h in (False, True)]

    mine = jnp.concatenate(coarse4(r3) + coarse4(acc[1, 1]), axis=0)
    own4[pl.ds(0, 4), :] = mine
    bcc[pl.ds(pl.multiple_of(8 * gy, 8), 4), :] = mine
    told(3)
    for dx, dy in line:
        remote(own4.at[pl.ds(0, 4), :], bcc.at[pl.ds(pl.multiple_of(8 * gy, 8), 4), :], GB, dx, dy)
    for dy in (1, -1):
        remote(v3s, halo3.at[1 - dy], H3, 0, dy)
    own2 = (pl.ds(HX[2], BX[2]), pl.ds(HY[2], BY[2]))
    sv2[0, own2[0], own2[1], :] = l2.s[own2[0], own2[1], :]
    sv2[1, own2[0], own2[1], :] = l2.vb[own2[0], own2[1], :]
    for q in range(2):
        send(l2.slabs(sv2.at[q], 4, 4), SV)

    received(GB)

    s4 = jnp.stack([bcc[pl.ds(h, ny, stride=8), :] for h in range(2)])
    k4 = jnp.stack([bcc[pl.ds(2 + h, ny, stride=8), :] for h in range(2)])
    shape = (2, ny, LANES)
    lane = lane_iota(shape)
    plane = lax.broadcasted_iota(jnp.int32, shape, 0)
    b1 = bit(lane, 1)
    y4, z4 = 2 * lax.broadcasted_iota(jnp.int32, shape, 1) + jnp.where(b1, 1, 0), lane >> 4
    lane2, row = lane_iota((ny, LANES)), lax.broadcasted_iota(jnp.int32, (ny, LANES), 0)
    c0 = bit(lane2, 0)

    def plus(t):
        return jnp.where(c0, ahead(t, 3), ahead(t, 1))

    def minus(t):
        return jnp.where(c0, ahead(t, -1), ahead(t, -3))

    def near4(v):
        up, down = ahead(v, 2), ahead(v, -2)
        return (
            jnp.stack([v[1], plus(v[0])]),
            jnp.stack([minus(v[1]), v[0]]),
            jnp.where(b1, rows_ahead(down, 1), up),
            jnp.where(b1, down, rows_ahead(up, -1)),
            ahead(v, 16),
            ahead(v, -16),
        )

    w4 = Whole(
        0.25**4,
        k4,
        near4,
        (
            (lane & 13 < 13) | (plane < 1),
            (lane & 13 > 0) | (plane > 0),
            y4 < 2 * ny - 1,
            y4 > 0,
            z4 < 7,
            z4 > 0,
        ),
    )

    def coarse5(t):
        t = t[0] + t[1]
        t = t + swap(t, 1)
        return 0.125 * (t + swap(t, 4))

    def near5(v):
        return plus(v), minus(v), rows_ahead(v, 1), rows_ahead(v, -1), ahead(v, 32), ahead(v, -32)

    x5, z5 = lane2 & 13, lane2 >> 5
    k5 = coarse5(k4)
    w5 = Whole(0.25**5, k5, near5, (x5 < 13, x5 > 0, row < ny - 1, row > 0, z5 < 3, z5 > 0))

    def coarse6(t):
        t = t + swap(t, 0)
        t = t + swap(t, 5)
        return 0.125 * (t + jnp.where((row & 1) != 0, rows_ahead(t, -1), rows_ahead(t, 1)))

    def near6(v):
        turned = ahead(v, 64)
        return ahead(v, 4), ahead(v, -4), rows_ahead(v, 2), rows_ahead(v, -2), turned, turned

    x6, z6 = (lane2 >> 2) & 3, lane2 >> 6
    w6 = Whole(0.25**6, coarse6(k5), near6, (x6 < 3, x6 > 0, row < ny - 2, row > 1, z6 < 1, z6 > 0))

    q4 = w4.inv * s4
    v4 = w4.sweep(q4, q4)
    q5 = w5.inv * coarse5(w4.residual(q4, v4))
    v5 = w5.sweep(q5, q5)
    q6 = w6.inv * coarse6(w5.residual(q5, v5))
    v6 = q6
    for _ in range(COARSE_SWEEPS - 1):
        v6 = w6.sweep(q6, v6)
    v5 = v5 + v6
    v5 = w5.sweep(q5, v5)
    v5 = w5.sweep(q5, v5)
    v4 = v4 + v5[None]
    v4 = w4.sweep(q4, v4)
    v4 = w4.sweep(q4, v4)
    v4s[:, pl.ds(8, ny), :] = v4

    received(H3)
    below = []
    for g in range(3):
        t = [jnp.broadcast_to(v4s[h, pl.ds(7 + gy + g, 1), :], (nx, LANES)) for h in range(2)]
        t = jnp.where(place, jnp.where(odd, t[1], t[0]), 0.0)
        for b in (0, 2, 3):
            t = t + swap(t, b)
        below.append(t)
    v = jnp.stack([halo3[0], v3s[...], halo3[2]]) + jnp.stack(below)
    v = jnp.where(in3, v, 0.0)
    v = w3.sweep(q3, v)
    v = w3.sweep(q3, v)
    v3u[:, pl.ds(8, nx), :] = v

    received(SV)
    shape = (8, LANES)
    lane, sub = lane_iota(shape), lax.broadcasted_iota(jnp.int32, shape, 0)
    for d in range(3):
        rows = [jnp.broadcast_to(v3u[g, pl.ds(7 + gx + d, 1), :], shape) for g in range(3)]
        rows = jnp.where(sub < 2, rows[0], jnp.where(sub < 6, rows[1], rows[2]))
        for xl in range(2):
            t = jnp.where((lane & 7) == 4 * xl + ((sub + 2) & 3), rows, 0.0)
            for b in range(3):
                t = t + swap(t, b)
            n = 2 * d + xl
            rep[n, pl.ds(0, 8, stride=2), :] = t
            rep[n, pl.ds(1, 8, stride=2), :] = t
            t = rep[n, pl.ds(0, EY[2]), :]
            for e in range(2):
                x = 2 * n + e
                l2.va[x] = jnp.where(l2.inside(x) > 0, sv2[1, x] + t, 0.0)
    l2.sweep(sv2.at[0], l2.va, l2.vb, 1, EX[2] - 1, unroll=99)
    l2.sweep(sv2.at[0], l2.vb, l2.va, 2, EX[2] - 2, unroll=99)

    def up1(i, c):
        t = l2.va[i + 2]
        rep[i, pl.ds(0, EY[2], stride=2), :] = t
        rep[i, pl.ds(1, EY[2], stride=2), :] = t
        t = rep[i, pl.ds(0, EY[1]), :]
        for e in range(2):
            x = 2 * i + 4 + e
            l1.va[x] = l1.vb[x] + t
        return c

    loop(0, 8, up1, 4)
    l1.sweep(l1.s, l1.va, l1.vb, 6, EX[1] - 6, 6)
    l1.sweep(l1.s, l1.vb, l1.va, 7, EX[1] - 7, 5)

    received(V0)
    all_of(V0).wait_send()
    row = lax.broadcasted_iota(jnp.int32, (EY[0], LANES), 0)
    mine0 = jnp.where((row >= HY[0]) & (row < HY[0] + BY[0]), 1.0, 0.0).astype(f32)

    def up0(i, c):
        t = l1.va[i + 7]
        rep[i, pl.ds(4, EY[1], stride=2), :] = t
        rep[i, pl.ds(5, EY[1], stride=2), :] = t
        t = rep[i, pl.ds(16, EY[0]), :]
        for e in range(2):
            x = 2 * i + 2 + e
            own = mine0 * jnp.where((x >= HX[0]) & (x < HX[0] + BX[0]), 1.0, 0.0).astype(f32)
            near = jnp.where(l0.inside(x) > 0, vh[x] + t, 0.0)
            l0.va[x] = jnp.where(own > 0, l0.vb[x] + t, near)
        return c

    loop(0, 10, up0, 5)
    l0.sweep(l0.s, l0.va, l0.vb, 3, EX[0] - 3, 9)
    def last(x, carry):
        c, near = l0.pull(l0.vb, x)
        t = KEEP * c + l0.inv[x] * (l0.s[x] + near)
        out[x - HX[0]] = t[HY[0] : HY[0] + BY[0]]
        return carry

    loop(HX[0], HX[0] + BX[0], last, 8)
    for phase in range(V0):
        all_of(phase).wait_send()


def solution(mesh):
    nx, ny = mesh.shape["gx"], mesh.shape["gy"]

    def body(defect, coefficient):
        dma = pltpu.SemaphoreType.DMA
        rows = phase_rows(nx, ny)
        scratch = []
        for l in range(3):
            scratch += [pltpu.VMEM((EX[l], EY[l], LANES), f32)] * 9
        scratch += [
            pltpu.VMEM((12, EY[0], LANES), f32),
            pltpu.VMEM((12, 72, LANES), f32),
            pltpu.VMEM((2, EX[2], EY[2], LANES), f32),
            pltpu.VMEM((EX[0], EY[0], LANES), f32),
            pltpu.VMEM((8, LANES), f32),
            pltpu.VMEM((2, 3, nx, LANES), f32),
            pltpu.VMEM((3, nx, LANES), f32),
            pltpu.VMEM((nx, LANES), f32),
            pltpu.VMEM((3, nx + 16, LANES), f32),
            pltpu.VMEM((8 * ny, LANES), f32),
            pltpu.VMEM((8, LANES), f32),
            pltpu.VMEM((2, ny + 16, LANES), f32),
            pltpu.VMEM((max(rows), LANES), f32),
            dma((2,)),
            dma((4,)),
            dma((len(rows),)),
            dma((len(rows),)),
            pltpu.SemaphoreType.REGULAR((4,)),
        ]
        return pl.pallas_call(
            functools.partial(kernel, nx, ny),
            out_shape=jax.ShapeDtypeStruct(defect.shape, f32),
            in_specs=[pl.BlockSpec(memory_space=pltpu.HBM)] * 2,
            out_specs=pl.BlockSpec(memory_space=pltpu.VMEM),
            scratch_shapes=scratch,
            compiler_params=pltpu.CompilerParams(
                collective_id=0, has_side_effects=True, vmem_limit_bytes=54784 << 10
            ),
        )(defect, coefficient)

    placed = P("gx", "gy", None)
    return jax.shard_map(
        body, mesh=mesh, in_specs=(placed, placed), out_specs=placed, check_vma=False
    )
```

```python
import functools

import jax
import jax.numpy as jnp
from jax import lax
from jax.experimental import pallas as pl
from jax.experimental.pallas import tpu as pltpu
from jax.sharding import PartitionSpec as P

MESH = pl.DeviceIdType.MESH
DAMP = 0.7
KEEP = 0.3
COARSE_SWEEPS = 8
LANES = 128
f32 = jnp.float32
U0W, U0S, U0R, U1W, U1S, U1R, U2W = 10, 9, 4, 11, 9, 4, 99

BX, BY = (16, 8, 4), (32, 16, 8)
HX, HY = (4, 8, 4), (4, 16, 8)
EX = tuple(b + 2 * h for b, h in zip(BX, HX))
EY = tuple(b + 2 * h for b, h in zip(BY, HY))

NEAR = [(1, 1), (1, -1), (-1, 1), (-1, -1), (1, 0), (-1, 0), (0, 1), (0, -1)]


def ahead(t, d):
    return pltpu.roll(t, (-d) % LANES, axis=t.ndim - 1)


def rows_ahead(t, d):
    n = t.shape[-2]
    return pltpu.roll(t, (-d) % n, axis=t.ndim - 2)


def planes_ahead(t, d):
    d = d % t.shape[0]
    return jnp.concatenate([t[d:], t[:d]], axis=0) if d else t


def lane_iota(shape):
    return lax.broadcasted_iota(jnp.int32, shape, len(shape) - 1)


def bit(lane, b):
    return (lane & (1 << b)) != 0


def swap(t, b):
    on = bit(lane_iota(t.shape), b)
    return jnp.where(on, ahead(t, -(1 << b)), ahead(t, 1 << b))


def spread(t, b, value):
    on = bit(lane_iota(t.shape), b)
    if value:
        return jnp.where(on, t, ahead(t, 1 << b))
    return jnp.where(on, ahead(t, -(1 << b)), t)


def loop(lo, hi, body, unroll=1, carry=()):
    rounds = (hi - lo) // unroll

    def step(r, c):
        for j in range(unroll):
            c = body(lo + unroll * r + j, c)
        return c

    if rounds > 1:
        carry = lax.fori_loop(0, rounds, step, carry)
    else:
        rounds = 0
    for i in range(lo + unroll * rounds, hi):
        carry = body(i, carry)
    return carry


ENTRY = NEAR + [(2, 0), (-2, 0)]
ROUNDS = (
    ((2, 0), (-2, 0), (0, 1), (0, -1)),
    ((4, 0), (-4, 0), (0, 2), (0, -2)),
    ((0, 4), (0, -4)),
    ((0, 8), (0, -8)),
)

K0, S0, K1, S1, GA, SV, GB, H3, K0Y, S0Y, S1Y, V0 = range(12)


def slabs(ref, halo, block, wide):
    parts = []
    for offset in NEAR:
        spans = []
        for d, h, b, w in zip(offset, halo, block, wide):
            if d == 0:
                spans.append((h, h, b))
            elif d > 0:
                spans.append((h + b - w, h - w, w))
            else:
                spans.append((h, h + b, w))
        (sx, tx, cx), (sy, ty, cy) = spans
        parts.append(
            (
                ref.at[pl.ds(sx, cx), pl.ds(sy, cy), :],
                ref.at[pl.ds(tx, cx), pl.ds(ty, cy), :],
            )
        )
    return parts


def both(low, high):
    return jnp.where(bit(lane_iota(low.shape), 0), high, low)


def apart(t):
    odd = bit(lane_iota(t.shape), 0)
    return jnp.where(odd, ahead(t, -1), t), jnp.where(odd, t, ahead(t, 1))


def phase_rows(nx, ny):
    def beside(level, wy):
        return BX[level] // (2 if level == 1 else 1) * 2 * wy

    def rim(level, wx, wy):
        bx, by = BX[level] // (2 if level == 1 else 1), BY[level]
        return (bx + 2 * wx) * (by + 2 * wy) - bx * by

    def ends(level, wx, wy):
        return rim(level, wx, wy) - beside(level, wy)

    return (
        ends(0, 3, 3),
        ends(0, 2, 2),
        rim(1, 4, 16),
        ends(1, 3, 14),
        5 * (nx - 1),
        2 * rim(2, 4, 4),
        4 * (ny - 1),
        4 * nx,
        beside(0, 3),
        beside(0, 2),
        beside(1, 14),
        rim(0, 2, 2),
    )


class Block:
    def __init__(self, level, gx, gy, nx, ny, refs):
        self.level = level
        self.factor = 0.25**level
        self.zs = 1 << level
        self.bx, self.by, self.hx, self.hy = BX[level], BY[level], HX[level], HY[level]
        self.ex, self.ey = EX[level], EY[level]
        self.gx, self.gy, self.nx, self.ny = gx, gy, nx, ny
        self.k, self.s, self.va, self.vb, self.wx, self.wy, self.wz, self.inv, self.dg = refs
        shape = (self.ey, LANES)
        self.lane = lane_iota(shape)
        y = gy * self.by - self.hy + lax.broadcasted_iota(jnp.int32, shape, 0)
        self.row_in = jnp.where((y >= 0) & (y < ny * self.by), 1.0, 0.0).astype(f32)

    def inside(self, x):
        gx = self.gx * self.bx - self.hx + x
        return self.row_in * jnp.where((gx >= 0) & (gx < self.nx * self.bx), 1.0, 0.0).astype(f32)

    def weights(self, lo, hi, unroll=1):
        half = 0.5 * self.factor
        last = self.lane >= LANES - self.zs
        first = self.lane < self.zs

        def step(x, carry):
            kc, fxm = carry
            m = self.inside(x)
            kn = self.k[x + 1] * self.inside(x + 1)
            fxp = half * (kc + kn)
            fyp = half * (kc + rows_ahead(kc, 1))
            fzp = half * (kc + jnp.where(last, 0.0, ahead(kc, self.zs)))
            wz = jnp.where(last, 0.0, fzp)
            fzm = jnp.where(first, half * kc, ahead(wz, -self.zs))
            diag = ((fxm + fxp) + (rows_ahead(fyp, -1) + fyp)) + (fzp + fzm)
            self.wx[x] = fxp
            self.wy[x] = fyp
            self.wz[x] = wz
            self.dg[x] = diag
            self.inv[x] = jnp.where(m > 0, DAMP / diag, 0.0)
            return kn, fxp

        k0 = self.k[lo - 1] * self.inside(lo - 1)
        k1 = self.k[lo] * self.inside(lo)
        self.wx[lo - 1] = half * (k0 + k1)
        loop(lo, hi, step, unroll, (k1, half * (k0 + k1)))

    def first(self, src, dst, lo, hi, unroll=1):
        def step(x, c):
            dst[x] = self.inv[x] * src[x]
            return c

        loop(lo, hi, step, unroll)

    def pull(self, v, x):
        c = v[x]
        wy, wz = self.wy[x], self.wz[x]
        t = self.wx[x] * v[x + 1] + self.wx[x - 1] * v[x - 1]
        u = wy * rows_ahead(c, 1) + rows_ahead(wy * c, -1)
        w = wz * ahead(c, self.zs) + ahead(wz * c, -self.zs)
        return c, (t + u) + w

    def sweep(self, s, src, dst, lo, hi, unroll=1, shift=0):
        def step(x, carry):
            c, near = self.pull(src, x)
            dst[x - shift] = KEEP * c + self.inv[x] * (s[x] + near)
            return carry

        loop(lo, hi, step, unroll)

    def residual(self, s, v, x):
        c, near = self.pull(v, x)
        return (s[x] - self.dg[x] * c) + near

    def restrict(self, plane, tmp, lo, pairs, row, count, put, unroll=1):
        lane = lane_iota((count, LANES))

        def step(i, c):
            x = lo + 2 * i
            t = plane(x) + plane(x + 1)
            tmp[i, pl.ds(0, t.shape[0]), :] = t
            t = tmp[i, pl.ds(row, count, stride=2), :] + tmp[i, pl.ds(row + 1, count, stride=2), :]
            put(i, 0.125 * (t + swap(t, self.level)))
            return c

        loop(0, pairs, step, unroll)


class Whole:
    def __init__(self, factor, k, near, masks, inside=None):
        half = 0.5 * factor
        self.near = near
        faces, parts = [], []
        for n, mask in zip(near(k), masks):
            face = half * (k + n)
            faces.append(jnp.where(mask, face, 0.0))
            parts.append(jnp.where(mask, face, half * k))
        diag = (parts[0] + parts[1]) + (parts[2] + parts[3]) + (parts[4] + parts[5])
        inv = DAMP / diag
        self.inv = inv if inside is None else jnp.where(inside, inv, 0.0)
        self.w = [face * self.inv for face in faces]
        self.back = diag * (1.0 / DAMP)

    def pull(self, v):
        t = [w * n for w, n in zip(self.w, self.near(v))]
        return (t[0] + t[1]) + (t[2] + t[3]) + (t[4] + t[5])

    def sweep(self, q, v):
        return (KEEP * v + q) + self.pull(v)

    def residual(self, q, v):
        return ((q - DAMP * v) + self.pull(v)) * self.back


def kernel(nx, ny, *refs):
    s_in, k_in, out = refs[:3]
    level_refs = [refs[3 + 9 * l : 12 + 9 * l] for l in range(3)]
    (
        tmp, rep, sv2, vh, k1p, s1p, pack, acc, halo3, v3s, v3u, bcc, own4, v4s, ruler,
        local_sem, out_sem, ssem, rsem, known,
    ) = refs[30:]
    gx, gy = lax.axis_index("gx"), lax.axis_index("gy")
    ROWS = phase_rows(nx, ny)

    def there(dx, dy):
        return (lax.rem(gx + dx + nx, nx), lax.rem(gy + dy + ny, ny))

    L = [Block(l, gx, gy, nx, ny, level_refs[l]) for l in range(3)]
    l0, l1, l2 = L
    own0 = (pl.ds(HX[0], BX[0]), pl.ds(HY[0], BY[0]))
    loads = [
        pltpu.make_async_copy(k_in, l0.k.at[own0[0], own0[1], :], local_sem.at[0]),
        pltpu.make_async_copy(s_in, l0.s.at[own0[0], own0[1], :], local_sem.at[1]),
    ]

    column = [(i, 0) for i in range(1, nx)]
    line = [(0, j) for j in range(1, ny)]
    line.sort(key=lambda o: -sum(min(c % 4, -c % 4) for c in (o[1] // 2, o[1] // 8)))
    column.sort(key=lambda o: -min(o[0], nx - o[0]))
    barrier = pltpu.get_barrier_semaphore()
    for dx, dy in ENTRY:
        pl.semaphore_signal(barrier, inc=1, device_id=there(dx, dy), device_id_type=MESH)
    for c in loads:
        c.start()
    v3u[...] = jnp.zeros_like(v3u)
    for c in loads:
        c.wait()

    half1 = (HX[1] // 2, HY[1]), (BX[1] // 2, BY[1])

    def put_k1(i, t):
        l1.k[HX[1] + i, pl.ds(HY[1], BY[1]), :] = t

    def pair_up(src, dst):
        for i in range(BX[1] // 2):
            x = HX[1] + 2 * i
            low, high = (src[x + j, pl.ds(HY[1], BY[1]), :] for j in range(2))
            dst[HX[1] // 2 + i, pl.ds(HY[1], BY[1]), :] = both(low, high)

    def split(src, dst, lo, hi, unroll):
        def step(i, c):
            dst[2 * i], dst[2 * i + 1] = apart(src[i])
            return c

        loop(lo, hi, step, unroll)

    l0.restrict(lambda x: l0.k[x, own0[1], :], tmp, HX[0], BX[1], 0, BY[1], put_k1, U0R)
    pair_up(l1.k, k1p)

    pl.semaphore_wait(barrier, len(ENTRY))

    def remote(src, dst, phase, dx, dy):
        c = pltpu.make_async_remote_copy(
            src, dst, ssem.at[phase], rsem.at[phase], device_id=there(dx, dy), device_id_type=MESH
        )
        c.start()

    def tell(step):
        for dx, dy in ROUNDS[step]:
            pl.semaphore_signal(known.at[step], inc=1, device_id=there(dx, dy), device_id_type=MESH)

    def told(step):
        pl.semaphore_wait(known.at[step], len(ROUNDS[step]))

    def all_of(phase):
        part = ruler.at[pl.ds(0, ROWS[phase]), :]
        return pltpu.make_async_remote_copy(
            part, part, ssem.at[phase], rsem.at[phase], device_id=there(1, 0), device_id_type=MESH
        )

    def received(phase):
        all_of(phase).wait_recv()

    def send(parts, phase, phase_y=None):
        for (dx, dy), (src, dst) in zip(NEAR, parts):
            remote(src, dst, phase if dx or phase_y is None else phase_y, dx, dy)

    tell(0)
    send(slabs(l0.k, (HX[0], HY[0]), (BX[0], BY[0]), (3, 3)), K0, K0Y)
    send(slabs(l0.s, (HX[0], HY[0]), (BX[0], BY[0]), (2, 2)), S0, S0Y)

    send(slabs(k1p, half1[0], half1[1], (4, 16)), K1)
    told(0)
    tell(1)

    def residual0(lo, pairs):
        def put(i, t):
            l1.s[HX[1] + (lo - HX[0]) // 2 + i, pl.ds(HY[1], BY[1]), :] = t

        l0.restrict(lambda x: l0.residual(l0.s, l0.vb, x), tmp, lo, pairs, HY[0], BY[1], put, 4)

    received(K0Y)
    l0.weights(5, 19, 7)
    received(S0Y)
    l0.first(l0.s, l0.va, 5, 19, 7)
    l0.sweep(l0.s, l0.va, l0.vb, 6, 18, 6)
    residual0(8, 4)
    received(K0)
    l0.weights(2, 5, 3)
    l0.weights(19, 22, 3)
    received(S0)
    l0.first(l0.s, l0.va, 2, 5, 3)
    l0.first(l0.s, l0.va, 19, 22, 3)
    l0.sweep(l0.s, l0.va, l0.vb, 3, 6, 3)
    l0.sweep(l0.s, l0.va, l0.vb, 18, 21, 3)
    residual0(4, 2)
    residual0(16, 2)
    pair_up(l1.s, s1p)
    send(slabs(s1p, half1[0], half1[1], (3, 14)), S1, S1Y)
    told(1)
    tell(2)
    for (dx, dy), (src, _), (_, dst) in zip(NEAR, slabs(l0.vb, (HX[0], HY[0]), (BX[0], BY[0]), (2, 2)), slabs(vh, (HX[0], HY[0]), (BX[0], BY[0]), (2, 2))):
        remote(src, dst, V0, dx, dy)

    received(K1)
    split(k1p, l1.k, 0, EX[1] // 2, 6)

    def put_k2(i, t):
        l2.k[i] = t

    l1.restrict(lambda x: l1.k[x], tmp, 0, EX[2], 0, EY[2], put_k2, 6)
    l1.weights(1, EX[1] - 1, U1W)
    l2.weights(1, EX[2] - 1, U2W)

    def packed(count, base, blocks):
        sub = lax.broadcasted_iota(jnp.int32, (count, LANES), 0)
        lane = lane_iota((count, LANES))
        low, high = (pack[i, pl.ds(0, count), :] for i in range(2))
        y = (sub + base) & 3
        t = jnp.where(lane & 7 == y, low, jnp.where(lane & 7 == 4 + y, high, 0.0))
        on = (lane & 3) == y
        return [jnp.sum(jnp.where(on & block(sub), t, 0.0), axis=0, keepdims=True) for block in blocks]

    def put_pack(i, t):
        pack[i, pl.ds(0, t.shape[0]), :] = t

    l2.restrict(lambda x: l2.k[x], tmp, HX[2], 2, 0, 12, put_pack, unroll=99)
    mine = pl.multiple_of(8 * gx, 8)
    blocks = [lambda r, g=g: (r >> 2) == g for g in range(3)]
    acc[pl.ds(mine + 2, 3), :] = jnp.concatenate(packed(16, 0, blocks), axis=0)

    def residual1(lo, pairs):
        def put(i, t):
            l2.s[lo // 2 + i] = t

        l1.restrict(lambda x: l1.residual(l1.s, l1.vb, x), tmp, lo, pairs, 0, EY[2], put, 3)

    received(S1Y)
    split(s1p, l1.s, 4, 8, 4)
    l1.first(l1.s, l1.va, 8, 16, 8)
    l1.sweep(l1.s, l1.va, l1.vb, 9, 15, 6)
    residual1(10, 2)
    received(S1)
    split(s1p, l1.s, 1, 4, 3)
    split(s1p, l1.s, 8, 11, 3)
    l1.first(l1.s, l1.va, 2, 8, 6)
    l1.first(l1.s, l1.va, 16, 22, 6)
    l1.sweep(l1.s, l1.va, l1.vb, 3, 9, 6)
    l1.sweep(l1.s, l1.va, l1.vb, 15, 21, 6)
    residual1(4, 3)
    residual1(14, 3)

    l2.first(l2.s, l2.va, 2, EX[2] - 2, unroll=99)
    l2.sweep(l2.s, l2.va, l2.vb, 3, EX[2] - 3, unroll=99)
    l2.restrict(lambda x: l2.residual(l2.s, l2.vb, x), tmp, HX[2], 2, HY[2] - 4, 8, put_pack, unroll=99)
    blocks = [lambda r: (r >= 2) & (r < 6), lambda r: (r < 2) | (r >= 6)]
    acc[pl.ds(mine, 2), :] = jnp.concatenate(packed(8, 2, blocks), axis=0)

    for dx, dy in column:
        remote(acc.at[pl.ds(mine, 5), :], acc.at[pl.ds(mine, 5), :], GA, dx, dy)

    told(2)
    tell(3)
    received(GA)

    shape = (3, nx, LANES)
    lane = lane_iota(shape)
    px = lax.broadcasted_iota(jnp.int32, shape, 1)
    py = gy - 1 + lax.broadcasted_iota(jnp.int32, shape, 0)
    b2, yl, z3 = bit(lane, 2), lane & 3, lane >> 3

    def near3(v):
        up, down = ahead(v, 4), ahead(v, -4)
        return (
            jnp.where(b2, rows_ahead(down, 1), up),
            jnp.where(b2, down, rows_ahead(up, -1)),
            jnp.where(yl == 3, planes_ahead(ahead(v, -3), 1), ahead(v, 1)),
            jnp.where(yl == 0, planes_ahead(ahead(v, 3), -1), ahead(v, -1)),
            ahead(v, 8),
            ahead(v, -8),
        )

    x3, y3 = 2 * px + jnp.where(b2, 1, 0), 4 * py + yl
    in3 = (py >= 0) & (py < ny)
    own3, side3, *k3 = (acc[pl.ds(q, nx, stride=8), :] for q in range(5))
    src3, k3 = jnp.stack([side3, own3, side3]), jnp.stack(k3)
    w3 = Whole(
        0.25**3,
        jnp.where(in3, k3, 0.0),
        near3,
        (x3 < 2 * nx - 1, x3 > 0, y3 < 4 * ny - 1, y3 > 0, z3 < 15, z3 > 0),
        in3,
    )
    q3 = w3.inv * src3
    v = w3.sweep(q3, q3)
    v3s[0], v3s[1] = v[1], own3
    r3 = w3.residual(q3, v)[1]

    shape = (nx, LANES)
    lane, sub = lane_iota(shape), lax.broadcasted_iota(jnp.int32, shape, 0)
    place = ((lane >> 1) & 6) + (lane & 1) == (sub >> 1)
    odd = (sub & 1) != 0

    def coarse4(t):
        t = t + swap(t, 2)
        t = t + swap(t, 0)
        t = 0.125 * (t + swap(t, 3))
        t = jnp.where(place, t, 0.0)
        return [jnp.sum(jnp.where(odd == h, t, 0.0), axis=0, keepdims=True) for h in (False, True)]

    mine4 = jnp.concatenate(coarse4(r3) + coarse4(k3[1]), axis=0)
    own4[pl.ds(0, 4), :] = mine4
    bcc[pl.ds(pl.multiple_of(8 * gy, 8), 4), :] = mine4
    told(3)
    for dx, dy in line:
        remote(own4.at[pl.ds(0, 4), :], bcc.at[pl.ds(pl.multiple_of(8 * gy, 8), 4), :], GB, dx, dy)
    for dy in (1, -1):
        remote(v3s, halo3.at[1 - dy], H3, 0, dy)
    own2 = (pl.ds(HX[2], BX[2]), pl.ds(HY[2], BY[2]))
    sv2[0, own2[0], own2[1], :] = l2.s[own2[0], own2[1], :]
    sv2[1, own2[0], own2[1], :] = l2.vb[own2[0], own2[1], :]
    for q in range(2):
        send(slabs(sv2.at[q], (HX[2], HY[2]), (BX[2], BY[2]), (4, 4)), SV)

    received(GB)

    s4 = jnp.stack([bcc[pl.ds(h, ny, stride=8), :] for h in range(2)])
    k4 = jnp.stack([bcc[pl.ds(2 + h, ny, stride=8), :] for h in range(2)])
    shape = (2, ny, LANES)
    lane = lane_iota(shape)
    plane = lax.broadcasted_iota(jnp.int32, shape, 0)
    b1 = bit(lane, 1)
    y4, z4 = 2 * lax.broadcasted_iota(jnp.int32, shape, 1) + jnp.where(b1, 1, 0), lane >> 4
    lane2, row = lane_iota((ny, LANES)), lax.broadcasted_iota(jnp.int32, (ny, LANES), 0)
    c0 = bit(lane2, 0)

    def plus(t):
        return jnp.where(c0, ahead(t, 3), ahead(t, 1))

    def minus(t):
        return jnp.where(c0, ahead(t, -1), ahead(t, -3))

    def near4(v):
        up, down = ahead(v, 2), ahead(v, -2)
        return (
            jnp.stack([v[1], plus(v[0])]),
            jnp.stack([minus(v[1]), v[0]]),
            jnp.where(b1, rows_ahead(down, 1), up),
            jnp.where(b1, down, rows_ahead(up, -1)),
            ahead(v, 16),
            ahead(v, -16),
        )

    w4 = Whole(
        0.25**4,
        k4,
        near4,
        (
            (lane & 13 < 13) | (plane < 1),
            (lane & 13 > 0) | (plane > 0),
            y4 < 2 * ny - 1,
            y4 > 0,
            z4 < 7,
            z4 > 0,
        ),
    )

    def coarse5(t):
        t = t[0] + t[1]
        t = t + swap(t, 1)
        return 0.125 * (t + swap(t, 4))

    def near5(v):
        return plus(v), minus(v), rows_ahead(v, 1), rows_ahead(v, -1), ahead(v, 32), ahead(v, -32)

    x5, z5 = lane2 & 13, lane2 >> 5
    k5 = coarse5(k4)
    w5 = Whole(0.25**5, k5, near5, (x5 < 13, x5 > 0, row < ny - 1, row > 0, z5 < 3, z5 > 0))

    def coarse6(t):
        t = t + swap(t, 0)
        t = t + swap(t, 5)
        return 0.125 * (t + jnp.where((row & 1) != 0, rows_ahead(t, -1), rows_ahead(t, 1)))

    def near6(v):
        turned = ahead(v, 64)
        return ahead(v, 4), ahead(v, -4), rows_ahead(v, 2), rows_ahead(v, -2), turned, turned

    x6, z6 = (lane2 >> 2) & 3, lane2 >> 6
    w6 = Whole(0.25**6, coarse6(k5), near6, (x6 < 3, x6 > 0, row < ny - 2, row > 1, z6 < 1, z6 > 0))

    q4 = w4.inv * s4
    v4 = w4.sweep(q4, q4)
    q5 = w5.inv * coarse5(w4.residual(q4, v4))
    v5 = w5.sweep(q5, q5)
    q6 = w6.inv * coarse6(w5.residual(q5, v5))
    v6 = q6
    for _ in range(COARSE_SWEEPS - 1):
        v6 = w6.sweep(q6, v6)
    v5 = v5 + v6
    v5 = w5.sweep(q5, v5)
    v5 = w5.sweep(q5, v5)
    v4 = v4 + v5[None]
    v4 = w4.sweep(q4, v4)
    v4 = w4.sweep(q4, v4)
    v4s[:, pl.ds(8, ny), :] = v4

    received(H3)
    below = []
    for g in range(3):
        t = [jnp.broadcast_to(v4s[h, pl.ds(7 + gy + g, 1), :], (nx, LANES)) for h in range(2)]
        t = jnp.where(place, jnp.where(odd, t[1], t[0]), 0.0)
        for b in (0, 2, 3):
            t = t + swap(t, b)
        below.append(t)
    q3 = w3.inv * jnp.stack([halo3[0, 1], own3, halo3[2, 1]])
    v = jnp.stack([halo3[0, 0], v3s[0], halo3[2, 0]]) + jnp.stack(below)
    v = jnp.where(in3, v, 0.0)
    v = w3.sweep(q3, v)
    v = w3.sweep(q3, v)
    v3u[:, pl.ds(8, nx), :] = v

    received(SV)
    shape = (8, LANES)
    lane, sub = lane_iota(shape), lax.broadcasted_iota(jnp.int32, shape, 0)
    for d in range(3):
        rows = [jnp.broadcast_to(v3u[g, pl.ds(7 + gx + d, 1), :], shape) for g in range(3)]
        rows = jnp.where(sub < 2, rows[0], jnp.where(sub < 6, rows[1], rows[2]))
        for xl in range(2):
            t = jnp.where((lane & 7) == 4 * xl + ((sub + 2) & 3), rows, 0.0)
            for b in range(3):
                t = t + swap(t, b)
            n = 2 * d + xl
            rep[n, pl.ds(4, 8, stride=2), :] = t
            rep[n, pl.ds(5, 8, stride=2), :] = t
            t = rep[n, pl.ds(0, EY[2]), :]
            for e in range(2):
                x = 2 * n + e
                l2.va[x] = jnp.where(l2.inside(x) > 0, sv2[1, x] + t, 0.0)
    l2.sweep(sv2.at[0], l2.va, l2.vb, 1, EX[2] - 1, unroll=99)
    l2.sweep(sv2.at[0], l2.vb, l2.va, 2, EX[2] - 2, unroll=99)

    def up1(i, c):
        t = l2.va[i + 2]
        rep[i, pl.ds(0, EY[2], stride=2), :] = t
        rep[i, pl.ds(1, EY[2], stride=2), :] = t
        t = rep[i, pl.ds(0, EY[1]), :]
        for e in range(2):
            x = 2 * i + 4 + e
            l1.va[x] = l1.vb[x] + t
        return c

    loop(0, 8, up1, 4)
    l1.sweep(l1.s, l1.va, l1.vb, 6, EX[1] - 6, 6)
    l1.sweep(l1.s, l1.vb, l1.va, 7, EX[1] - 7, 5)

    received(V0)
    all_of(V0).wait_send()
    row = lax.broadcasted_iota(jnp.int32, (EY[0], LANES), 0)
    mine0 = jnp.where((row >= HY[0]) & (row < HY[0] + BY[0]), 1.0, 0.0).astype(f32)

    def up0(i, c):
        t = l1.va[i + 7, pl.ds(8, 32), :]
        rep[i, pl.ds(4, 32, stride=2), :] = t
        rep[i, pl.ds(5, 32, stride=2), :] = t
        t = rep[i, pl.ds(16, EY[0]), :]
        for e in range(2):
            x = 2 * i + 2 + e
            own = mine0 * jnp.where((x >= HX[0]) & (x < HX[0] + BX[0]), 1.0, 0.0).astype(f32)
            near = jnp.where(l0.inside(x) > 0, vh[x] + t, 0.0)
            l0.va[x] = jnp.where(own > 0, l0.vb[x] + t, near)
        return c

    loop(0, 10, up0, 5)
    l0.sweep(l0.s, l0.va, l0.vb, 3, EX[0] - 3, 9)
    def last(x, carry):
        c, near = l0.pull(l0.vb, x)
        t = KEEP * c + l0.inv[x] * (l0.s[x] + near)
        out[x - HX[0]] = t[HY[0] : HY[0] + BY[0]]
        return carry

    loop(HX[0], HX[0] + BX[0], last, 8)
    for phase in range(V0):
        all_of(phase).wait_send()


def solution(mesh):
    nx, ny = mesh.shape["gx"], mesh.shape["gy"]

    def body(defect, coefficient):
        dma = pltpu.SemaphoreType.DMA
        rows = phase_rows(nx, ny)
        scratch = []
        for l in range(3):
            scratch += [pltpu.VMEM((EX[l], EY[l], LANES), f32)] * 9
        scratch += [
            pltpu.VMEM((12, EY[1], LANES), f32),
            pltpu.VMEM((12, 72, LANES), f32),
            pltpu.VMEM((2, EX[2], EY[2], LANES), f32),
            pltpu.VMEM((EX[0], EY[0], LANES), f32),
            pltpu.VMEM((EX[1] // 2, EY[1], LANES), f32),
            pltpu.VMEM((EX[1] // 2, EY[1], LANES), f32),
            pltpu.VMEM((2, 16, LANES), f32),
            pltpu.VMEM((8 * nx, LANES), f32),
            pltpu.VMEM((3, 2, nx, LANES), f32),
            pltpu.VMEM((2, nx, LANES), f32),
            pltpu.VMEM((3, nx + 16, LANES), f32),
            pltpu.VMEM((8 * ny, LANES), f32),
            pltpu.VMEM((8, LANES), f32),
            pltpu.VMEM((2, ny + 16, LANES), f32),
            pltpu.VMEM((max(rows), LANES), f32),
            dma((2,)),
            dma((4,)),
            dma((len(rows),)),
            dma((len(rows),)),
            pltpu.SemaphoreType.REGULAR((4,)),
        ]
        return pl.pallas_call(
            functools.partial(kernel, nx, ny),
            out_shape=jax.ShapeDtypeStruct(defect.shape, f32),
            in_specs=[pl.BlockSpec(memory_space=pltpu.HBM)] * 2,
            out_specs=pl.BlockSpec(memory_space=pltpu.VMEM),
            scratch_shapes=scratch,
            compiler_params=pltpu.CompilerParams(
                collective_id=0, has_side_effects=True, vmem_limit_bytes=54784 << 10
            ),
        )(defect, coefficient)

    placed = P("gx", "gy", None)
    return jax.shard_map(
        body, mesh=mesh, in_specs=(placed, placed), out_specs=placed, check_vma=False
    )
```

```python
import functools

import jax
import jax.numpy as jnp
from jax import lax
from jax.experimental import pallas as pl
from jax.experimental.pallas import tpu as pltpu
from jax.sharding import PartitionSpec as P

MESH = pl.DeviceIdType.MESH
DAMP = 0.7
KEEP = 0.3
COARSE_SWEEPS = 8
LANES = 128
f32 = jnp.float32
U0W, U0S, U0R, U1W, U1S, U1R, U2W = 10, 9, 4, 11, 9, 4, 99

BX, BY = (16, 8, 4), (32, 16, 8)
HX, HY = (4, 8, 4), (4, 16, 8)
EX = tuple(b + 2 * h for b, h in zip(BX, HX))
EY = tuple(b + 2 * h for b, h in zip(BY, HY))

NEAR = [(1, 1), (1, -1), (-1, 1), (-1, -1), (1, 0), (-1, 0), (0, 1), (0, -1)]


def ahead(t, d):
    return pltpu.roll(t, (-d) % LANES, axis=t.ndim - 1)


def rows_ahead(t, d):
    n = t.shape[-2]
    return pltpu.roll(t, (-d) % n, axis=t.ndim - 2)


def planes_ahead(t, d):
    d = d % t.shape[0]
    return jnp.concatenate([t[d:], t[:d]], axis=0) if d else t


def lane_iota(shape):
    return lax.broadcasted_iota(jnp.int32, shape, len(shape) - 1)


def bit(lane, b):
    return (lane & (1 << b)) != 0


def swap(t, b):
    on = bit(lane_iota(t.shape), b)
    return jnp.where(on, ahead(t, -(1 << b)), ahead(t, 1 << b))


def spread(t, b, value):
    on = bit(lane_iota(t.shape), b)
    if value:
        return jnp.where(on, t, ahead(t, 1 << b))
    return jnp.where(on, ahead(t, -(1 << b)), t)


def loop(lo, hi, body, unroll=1, carry=()):
    rounds = (hi - lo) // unroll

    def step(r, c):
        for j in range(unroll):
            c = body(lo + unroll * r + j, c)
        return c

    if rounds > 1:
        carry = lax.fori_loop(0, rounds, step, carry)
    else:
        rounds = 0
    for i in range(lo + unroll * rounds, hi):
        carry = body(i, carry)
    return carry


ENTRY = NEAR + [(2, 0), (-2, 0)]
ROUNDS = (
    ((2, 0), (-2, 0), (0, 1), (0, -1)),
    ((4, 0), (-4, 0), (0, 2), (0, -2)),
    ((0, 4), (0, -4)),
    ((0, 8), (0, -8)),
)

K0, S0, K1, S1, GA, SV, GB, H3, K0Y, S0Y, S1Y, GK, KB, V0 = range(14)


def slabs(ref, halo, block, wide):
    parts = []
    for offset in NEAR:
        spans = []
        for d, h, b, w in zip(offset, halo, block, wide):
            if d == 0:
                spans.append((h, h, b))
            elif d > 0:
                spans.append((h + b - w, h - w, w))
            else:
                spans.append((h, h + b, w))
        (sx, tx, cx), (sy, ty, cy) = spans
        parts.append(
            (
                ref.at[pl.ds(sx, cx), pl.ds(sy, cy), :],
                ref.at[pl.ds(tx, cx), pl.ds(ty, cy), :],
            )
        )
    return parts


def both(low, high):
    return jnp.where(bit(lane_iota(low.shape), 0), high, low)


def apart(t):
    odd = bit(lane_iota(t.shape), 0)
    return jnp.where(odd, ahead(t, -1), t), jnp.where(odd, t, ahead(t, 1))


def phase_rows(nx, ny):
    def beside(level, wy):
        return BX[level] // (2 if level == 1 else 1) * 2 * wy

    def rim(level, wx, wy):
        bx, by = BX[level] // (2 if level == 1 else 1), BY[level]
        return (bx + 2 * wx) * (by + 2 * wy) - bx * by

    def ends(level, wx, wy):
        return rim(level, wx, wy) - beside(level, wy)

    return (
        ends(0, 3, 3),
        ends(0, 2, 2),
        rim(1, 4, 16),
        ends(1, 3, 14),
        2 * (nx - 1),
        2 * rim(2, 4, 4),
        2 * (ny - 1),
        4 * nx,
        beside(0, 3),
        beside(0, 2),
        beside(1, 14),
        3 * (nx - 1),
        2 * (ny - 1),
        rim(0, 2, 2),
    )


class Block:
    def __init__(self, level, gx, gy, nx, ny, refs):
        self.level = level
        self.factor = 0.25**level
        self.zs = 1 << level
        self.bx, self.by, self.hx, self.hy = BX[level], BY[level], HX[level], HY[level]
        self.ex, self.ey = EX[level], EY[level]
        self.gx, self.gy, self.nx, self.ny = gx, gy, nx, ny
        self.k, self.s, self.va, self.vb, self.wx, self.wy, self.wz, self.inv, self.dg = refs
        shape = (self.ey, LANES)
        self.lane = lane_iota(shape)
        y = gy * self.by - self.hy + lax.broadcasted_iota(jnp.int32, shape, 0)
        self.row_in = jnp.where((y >= 0) & (y < ny * self.by), 1.0, 0.0).astype(f32)

    def inside(self, x):
        gx = self.gx * self.bx - self.hx + x
        return self.row_in * jnp.where((gx >= 0) & (gx < self.nx * self.bx), 1.0, 0.0).astype(f32)

    def weights(self, lo, hi, unroll=1):
        half = 0.5 * self.factor
        last = self.lane >= LANES - self.zs
        first = self.lane < self.zs

        def step(x, carry):
            kc, fxm = carry
            m = self.inside(x)
            kn = self.k[x + 1] * self.inside(x + 1)
            fxp = half * (kc + kn)
            fyp = half * (kc + rows_ahead(kc, 1))
            fzp = half * (kc + jnp.where(last, 0.0, ahead(kc, self.zs)))
            wz = jnp.where(last, 0.0, fzp)
            fzm = jnp.where(first, half * kc, ahead(wz, -self.zs))
            diag = ((fxm + fxp) + (rows_ahead(fyp, -1) + fyp)) + (fzp + fzm)
            self.wx[x] = fxp
            self.wy[x] = fyp
            self.wz[x] = wz
            self.dg[x] = diag
            self.inv[x] = jnp.where(m > 0, DAMP / diag, 0.0)
            return kn, fxp

        k0 = self.k[lo - 1] * self.inside(lo - 1)
        k1 = self.k[lo] * self.inside(lo)
        self.wx[lo - 1] = half * (k0 + k1)
        loop(lo, hi, step, unroll, (k1, half * (k0 + k1)))

    def first(self, src, dst, lo, hi, unroll=1):
        def step(x, c):
            dst[x] = self.inv[x] * src[x]
            return c

        loop(lo, hi, step, unroll)

    def pull(self, v, x):
        c = v[x]
        wy, wz = self.wy[x], self.wz[x]
        t = self.wx[x] * v[x + 1] + self.wx[x - 1] * v[x - 1]
        u = wy * rows_ahead(c, 1) + rows_ahead(wy * c, -1)
        w = wz * ahead(c, self.zs) + ahead(wz * c, -self.zs)
        return c, (t + u) + w

    def sweep(self, s, src, dst, lo, hi, unroll=1, shift=0):
        def step(x, carry):
            c, near = self.pull(src, x)
            dst[x - shift] = KEEP * c + self.inv[x] * (s[x] + near)
            return carry

        loop(lo, hi, step, unroll)

    def residual(self, s, v, x):
        c, near = self.pull(v, x)
        return (s[x] - self.dg[x] * c) + near

    def restrict(self, plane, tmp, lo, pairs, row, count, put, unroll=1):
        lane = lane_iota((count, LANES))

        def step(i, c):
            x = lo + 2 * i
            t = plane(x) + plane(x + 1)
            tmp[i, pl.ds(0, t.shape[0]), :] = t
            t = tmp[i, pl.ds(row, count, stride=2), :] + tmp[i, pl.ds(row + 1, count, stride=2), :]
            put(i, 0.125 * (t + swap(t, self.level)))
            return c

        loop(0, pairs, step, unroll)


class Whole:
    def __init__(self, factor, k, near, masks, inside=None):
        half = 0.5 * factor
        self.near = near
        faces, parts = [], []
        for n, mask in zip(near(k), masks):
            face = half * (k + n)
            faces.append(jnp.where(mask, face, 0.0))
            parts.append(jnp.where(mask, face, half * k))
        diag = (parts[0] + parts[1]) + (parts[2] + parts[3]) + (parts[4] + parts[5])
        inv = DAMP / diag
        self.inv = inv if inside is None else jnp.where(inside, inv, 0.0)
        self.w = [face * self.inv for face in faces]
        self.back = diag * (1.0 / DAMP)

    def pull(self, v):
        t = [w * n for w, n in zip(self.w, self.near(v))]
        return (t[0] + t[1]) + (t[2] + t[3]) + (t[4] + t[5])

    def sweep(self, q, v):
        return (KEEP * v + q) + self.pull(v)

    def residual(self, q, v):
        return ((q - DAMP * v) + self.pull(v)) * self.back


def kernel(nx, ny, *refs):
    s_in, k_in, out = refs[:3]
    level_refs = [refs[3 + 9 * l : 12 + 9 * l] for l in range(3)]
    (
        tmp, rep, sv2, vh, k1p, s1p, pack, acc, acck, halo3, v3s, v3u, bcs, bck, own4, v4s, ruler,
        local_sem, out_sem, ssem, rsem, known,
    ) = refs[30:]
    gx, gy = lax.axis_index("gx"), lax.axis_index("gy")
    ROWS = phase_rows(nx, ny)

    def there(dx, dy):
        return (lax.rem(gx + dx + nx, nx), lax.rem(gy + dy + ny, ny))

    L = [Block(l, gx, gy, nx, ny, level_refs[l]) for l in range(3)]
    l0, l1, l2 = L
    own0 = (pl.ds(HX[0], BX[0]), pl.ds(HY[0], BY[0]))
    loads = [
        pltpu.make_async_copy(k_in, l0.k.at[own0[0], own0[1], :], local_sem.at[0]),
        pltpu.make_async_copy(s_in, l0.s.at[own0[0], own0[1], :], local_sem.at[1]),
    ]

    column = [(i, 0) for i in range(1, nx)]
    line = [(0, j) for j in range(1, ny)]
    line.sort(key=lambda o: -sum(min(c % 4, -c % 4) for c in (o[1] // 2, o[1] // 8)))
    column.sort(key=lambda o: -min(o[0], nx - o[0]))
    barrier = pltpu.get_barrier_semaphore()
    for dx, dy in ENTRY:
        pl.semaphore_signal(barrier, inc=1, device_id=there(dx, dy), device_id_type=MESH)
    for c in loads:
        c.start()
    v3u[...] = jnp.zeros_like(v3u)
    for c in loads:
        c.wait()

    half1 = (HX[1] // 2, HY[1]), (BX[1] // 2, BY[1])

    def put_k1(i, t):
        l1.k[HX[1] + i, pl.ds(HY[1], BY[1]), :] = t

    def pair_up(src, dst):
        for i in range(BX[1] // 2):
            x = HX[1] + 2 * i
            low, high = (src[x + j, pl.ds(HY[1], BY[1]), :] for j in range(2))
            dst[HX[1] // 2 + i, pl.ds(HY[1], BY[1]), :] = both(low, high)

    def split(src, dst, lo, hi, unroll, start=False):
        def step(i, c):
            for x, t in zip((2 * i, 2 * i + 1), apart(src[i])):
                dst[x] = t
                if start:
                    l1.va[x] = l1.inv[x] * t
            return c

        loop(lo, hi, step, unroll)

    l0.restrict(lambda x: l0.k[x, own0[1], :], tmp, HX[0], BX[1], 0, BY[1], put_k1, U0R)
    pair_up(l1.k, k1p)

    pl.semaphore_wait(barrier, len(ENTRY))

    def remote(src, dst, phase, dx, dy):
        c = pltpu.make_async_remote_copy(
            src, dst, ssem.at[phase], rsem.at[phase], device_id=there(dx, dy), device_id_type=MESH
        )
        c.start()

    def tell(step):
        for dx, dy in ROUNDS[step]:
            pl.semaphore_signal(known.at[step], inc=1, device_id=there(dx, dy), device_id_type=MESH)

    def told(step):
        pl.semaphore_wait(known.at[step], len(ROUNDS[step]))

    def all_of(phase):
        part = ruler.at[pl.ds(0, ROWS[phase]), :]
        return pltpu.make_async_remote_copy(
            part, part, ssem.at[phase], rsem.at[phase], device_id=there(1, 0), device_id_type=MESH
        )

    def received(phase):
        all_of(phase).wait_recv()

    def send(parts, phase, phase_y=None):
        for (dx, dy), (src, dst) in zip(NEAR, parts):
            remote(src, dst, phase if dx or phase_y is None else phase_y, dx, dy)

    tell(0)
    send(slabs(l0.k, (HX[0], HY[0]), (BX[0], BY[0]), (3, 3)), K0, K0Y)
    send(slabs(l0.s, (HX[0], HY[0]), (BX[0], BY[0]), (2, 2)), S0, S0Y)

    send(slabs(k1p, half1[0], half1[1], (4, 16)), K1)
    told(0)
    tell(1)

    def residual0(lo, pairs):
        def put(i, t):
            l1.s[HX[1] + (lo - HX[0]) // 2 + i, pl.ds(HY[1], BY[1]), :] = t

        l0.restrict(lambda x: l0.residual(l0.s, l0.vb, x), tmp, lo, pairs, HY[0], BY[1], put, 4)

    received(K0Y)
    l0.weights(5, 19, 7)
    received(S0Y)
    l0.first(l0.s, l0.va, 5, 19, 7)
    l0.sweep(l0.s, l0.va, l0.vb, 6, 18, 6)
    residual0(8, 4)
    received(K0)
    l0.weights(2, 5, 3)
    l0.weights(19, 22, 3)
    received(S0)
    l0.first(l0.s, l0.va, 2, 5, 3)
    l0.first(l0.s, l0.va, 19, 22, 3)
    l0.sweep(l0.s, l0.va, l0.vb, 3, 6, 3)
    l0.sweep(l0.s, l0.va, l0.vb, 18, 21, 3)
    residual0(4, 2)
    residual0(16, 2)
    pair_up(l1.s, s1p)
    send(slabs(s1p, half1[0], half1[1], (3, 14)), S1, S1Y)
    told(1)
    tell(2)
    received(K1)
    split(k1p, l1.k, 0, EX[1] // 2, 6)

    def put_k2(i, t):
        l2.k[i] = t

    l1.restrict(lambda x: l1.k[x], tmp, 0, EX[2], 0, EY[2], put_k2, 6)
    l1.weights(1, EX[1] - 1, U1W)
    l2.weights(1, EX[2] - 1, U2W)

    def packed(count, base, blocks):
        sub = lax.broadcasted_iota(jnp.int32, (count, LANES), 0)
        lane = lane_iota((count, LANES))
        low, high = (pack[i, pl.ds(0, count), :] for i in range(2))
        y = (sub + base) & 3
        t = jnp.where(lane & 7 == y, low, jnp.where(lane & 7 == 4 + y, high, 0.0))
        on = (lane & 3) == y
        return [jnp.sum(jnp.where(on & block(sub), t, 0.0), axis=0, keepdims=True) for block in blocks]

    def put_pack(i, t):
        pack[i, pl.ds(0, t.shape[0]), :] = t

    l2.restrict(lambda x: l2.k[x], tmp, HX[2], 2, 0, 12, put_pack, unroll=99)
    mine = pl.multiple_of(8 * gx, 8)
    blocks = [lambda r, g=g: (r >> 2) == g for g in range(3)]
    acck[pl.ds(mine, 3), :] = jnp.concatenate(packed(16, 0, blocks), axis=0)
    for dx, dy in column:
        remote(acck.at[pl.ds(mine, 3), :], acck.at[pl.ds(mine, 3), :], GK, dx, dy)

    def residual1(lo, pairs):
        def put(i, t):
            l2.s[lo // 2 + i] = t

        l1.restrict(lambda x: l1.residual(l1.s, l1.vb, x), tmp, lo, pairs, 0, EY[2], put, 3)

    received(S1Y)
    split(s1p, l1.s, 4, 8, 4, start=True)
    l1.sweep(l1.s, l1.va, l1.vb, 9, 15, 6)
    residual1(10, 2)
    received(S1)
    split(s1p, l1.s, 1, 4, 3, start=True)
    split(s1p, l1.s, 8, 11, 3, start=True)
    l1.sweep(l1.s, l1.va, l1.vb, 3, 9, 6)
    l1.sweep(l1.s, l1.va, l1.vb, 15, 21, 6)
    residual1(4, 3)
    residual1(14, 3)

    l2.first(l2.s, l2.va, 2, EX[2] - 2, unroll=99)
    l2.sweep(l2.s, l2.va, l2.vb, 3, EX[2] - 3, unroll=99)
    l2.restrict(lambda x: l2.residual(l2.s, l2.vb, x), tmp, HX[2], 2, HY[2] - 4, 8, put_pack, unroll=99)
    blocks = [lambda r: (r >= 2) & (r < 6), lambda r: (r < 2) | (r >= 6)]
    acc[pl.ds(mine, 2), :] = jnp.concatenate(packed(8, 2, blocks), axis=0)

    for dx, dy in column:
        remote(acc.at[pl.ds(mine, 2), :], acc.at[pl.ds(mine, 2), :], GA, dx, dy)

    told(2)
    tell(3)
    received(GK)

    shape = (3, nx, LANES)
    lane = lane_iota(shape)
    px = lax.broadcasted_iota(jnp.int32, shape, 1)
    py = gy - 1 + lax.broadcasted_iota(jnp.int32, shape, 0)
    b2, yl, z3 = bit(lane, 2), lane & 3, lane >> 3

    def near3(v):
        up, down = ahead(v, 4), ahead(v, -4)
        return (
            jnp.where(b2, rows_ahead(down, 1), up),
            jnp.where(b2, down, rows_ahead(up, -1)),
            jnp.where(yl == 3, planes_ahead(ahead(v, -3), 1), ahead(v, 1)),
            jnp.where(yl == 0, planes_ahead(ahead(v, 3), -1), ahead(v, -1)),
            ahead(v, 8),
            ahead(v, -8),
        )

    x3, y3 = 2 * px + jnp.where(b2, 1, 0), 4 * py + yl
    in3 = (py >= 0) & (py < ny)
    k3 = jnp.stack([acck[pl.ds(q, nx, stride=8), :] for q in range(3)])
    w3 = Whole(
        0.25**3,
        jnp.where(in3, k3, 0.0),
        near3,
        (x3 < 2 * nx - 1, x3 > 0, y3 < 4 * ny - 1, y3 > 0, z3 < 15, z3 > 0),
        in3,
    )
    shape = (nx, LANES)
    lane, sub = lane_iota(shape), lax.broadcasted_iota(jnp.int32, shape, 0)
    place = ((lane >> 1) & 6) + (lane & 1) == (sub >> 1)
    odd = (sub & 1) != 0

    def coarse4(t):
        t = t + swap(t, 2)
        t = t + swap(t, 0)
        t = 0.125 * (t + swap(t, 3))
        t = jnp.where(place, t, 0.0)
        return [jnp.sum(jnp.where(odd == h, t, 0.0), axis=0, keepdims=True) for h in (False, True)]

    def share4(rows, first, bcc, phase):
        own4[pl.ds(first, 2), :] = rows
        there4 = pl.ds(pl.multiple_of(8 * gy, 8), 2)
        bcc[there4, :] = rows
        for dx, dy in line:
            remote(own4.at[pl.ds(first, 2), :], bcc.at[there4, :], phase, dx, dy)

    told(3)
    share4(jnp.concatenate(coarse4(k3[1]), axis=0), 2, bck, KB)

    received(GA)
    own3, side3 = (acc[pl.ds(q, nx, stride=8), :] for q in range(2))
    src3 = jnp.stack([side3, own3, side3])
    q3 = w3.inv * src3
    v = w3.sweep(q3, q3)
    v3s[0], v3s[1] = v[1], own3
    r3 = w3.residual(q3, v)[1]

    share4(jnp.concatenate(coarse4(r3), axis=0), 0, bcs, GB)
    for dy in (1, -1):
        remote(v3s, halo3.at[1 - dy], H3, 0, dy)
    for (dx, dy), (src, _), (_, dst) in zip(NEAR, slabs(l0.vb, (HX[0], HY[0]), (BX[0], BY[0]), (2, 2)), slabs(vh, (HX[0], HY[0]), (BX[0], BY[0]), (2, 2))):
        remote(src, dst, V0, dx, dy)

    own2 = (pl.ds(HX[2], BX[2]), pl.ds(HY[2], BY[2]))
    sv2[0, own2[0], own2[1], :] = l2.s[own2[0], own2[1], :]
    sv2[1, own2[0], own2[1], :] = l2.vb[own2[0], own2[1], :]
    for q in range(2):
        send(slabs(sv2.at[q], (HX[2], HY[2]), (BX[2], BY[2]), (4, 4)), SV)

    received(KB)

    k4 = jnp.stack([bck[pl.ds(h, ny, stride=8), :] for h in range(2)])
    shape = (2, ny, LANES)
    lane = lane_iota(shape)
    plane = lax.broadcasted_iota(jnp.int32, shape, 0)
    b1 = bit(lane, 1)
    y4, z4 = 2 * lax.broadcasted_iota(jnp.int32, shape, 1) + jnp.where(b1, 1, 0), lane >> 4
    lane2, row = lane_iota((ny, LANES)), lax.broadcasted_iota(jnp.int32, (ny, LANES), 0)
    c0 = bit(lane2, 0)

    def plus(t):
        return jnp.where(c0, ahead(t, 3), ahead(t, 1))

    def minus(t):
        return jnp.where(c0, ahead(t, -1), ahead(t, -3))

    def near4(v):
        up, down = ahead(v, 2), ahead(v, -2)
        return (
            jnp.stack([v[1], plus(v[0])]),
            jnp.stack([minus(v[1]), v[0]]),
            jnp.where(b1, rows_ahead(down, 1), up),
            jnp.where(b1, down, rows_ahead(up, -1)),
            ahead(v, 16),
            ahead(v, -16),
        )

    w4 = Whole(
        0.25**4,
        k4,
        near4,
        (
            (lane & 13 < 13) | (plane < 1),
            (lane & 13 > 0) | (plane > 0),
            y4 < 2 * ny - 1,
            y4 > 0,
            z4 < 7,
            z4 > 0,
        ),
    )

    def coarse5(t):
        t = t[0] + t[1]
        t = t + swap(t, 1)
        return 0.125 * (t + swap(t, 4))

    def near5(v):
        return plus(v), minus(v), rows_ahead(v, 1), rows_ahead(v, -1), ahead(v, 32), ahead(v, -32)

    x5, z5 = lane2 & 13, lane2 >> 5
    k5 = coarse5(k4)
    w5 = Whole(0.25**5, k5, near5, (x5 < 13, x5 > 0, row < ny - 1, row > 0, z5 < 3, z5 > 0))

    def coarse6(t):
        t = t + swap(t, 0)
        t = t + swap(t, 5)
        return 0.125 * (t + jnp.where((row & 1) != 0, rows_ahead(t, -1), rows_ahead(t, 1)))

    def near6(v):
        turned = ahead(v, 64)
        return ahead(v, 4), ahead(v, -4), rows_ahead(v, 2), rows_ahead(v, -2), turned, turned

    x6, z6 = (lane2 >> 2) & 3, lane2 >> 6
    w6 = Whole(0.25**6, coarse6(k5), near6, (x6 < 3, x6 > 0, row < ny - 2, row > 1, z6 < 1, z6 > 0))

    received(GB)
    s4 = jnp.stack([bcs[pl.ds(h, ny, stride=8), :] for h in range(2)])
    q4 = w4.inv * s4
    v4 = w4.sweep(q4, q4)
    q5 = w5.inv * coarse5(w4.residual(q4, v4))
    v5 = w5.sweep(q5, q5)
    q6 = w6.inv * coarse6(w5.residual(q5, v5))
    v6 = q6
    for _ in range(COARSE_SWEEPS - 1):
        v6 = w6.sweep(q6, v6)
    v5 = v5 + v6
    v5 = w5.sweep(q5, v5)
    v5 = w5.sweep(q5, v5)
    v4 = v4 + v5[None]
    v4 = w4.sweep(q4, v4)
    v4 = w4.sweep(q4, v4)
    v4s[:, pl.ds(8, ny), :] = v4

    received(H3)
    below = []
    for g in range(3):
        t = [jnp.broadcast_to(v4s[h, pl.ds(7 + gy + g, 1), :], (nx, LANES)) for h in range(2)]
        t = jnp.where(place, jnp.where(odd, t[1], t[0]), 0.0)
        for b in (0, 2, 3):
            t = t + swap(t, b)
        below.append(t)
    q3 = w3.inv * jnp.stack([halo3[0, 1], own3, halo3[2, 1]])
    v = jnp.stack([halo3[0, 0], v3s[0], halo3[2, 0]]) + jnp.stack(below)
    v = jnp.where(in3, v, 0.0)
    v = w3.sweep(q3, v)
    v = w3.sweep(q3, v)
    v3u[:, pl.ds(8, nx), :] = v

    received(SV)
    shape = (8, LANES)
    lane, sub = lane_iota(shape), lax.broadcasted_iota(jnp.int32, shape, 0)
    for d in range(3):
        rows = [jnp.broadcast_to(v3u[g, pl.ds(7 + gx + d, 1), :], shape) for g in range(3)]
        rows = jnp.where(sub < 2, rows[0], jnp.where(sub < 6, rows[1], rows[2]))
        for xl in range(2):
            t = jnp.where((lane & 7) == 4 * xl + ((sub + 2) & 3), rows, 0.0)
            for b in range(3):
                t = t + swap(t, b)
            n = 2 * d + xl
            rep[n, pl.ds(4, 8, stride=2), :] = t
            rep[n, pl.ds(5, 8, stride=2), :] = t
            t = rep[n, pl.ds(0, EY[2]), :]
            for e in range(2):
                x = 2 * n + e
                l2.va[x] = jnp.where(l2.inside(x) > 0, sv2[1, x] + t, 0.0)
    l2.sweep(sv2.at[0], l2.va, l2.vb, 1, EX[2] - 1, unroll=99)
    l2.sweep(sv2.at[0], l2.vb, l2.va, 2, EX[2] - 2, unroll=99)

    def up1(i, c):
        t = l2.va[i + 2]
        rep[i, pl.ds(0, EY[2], stride=2), :] = t
        rep[i, pl.ds(1, EY[2], stride=2), :] = t
        t = rep[i, pl.ds(0, EY[1]), :]
        for e in range(2):
            x = 2 * i + 4 + e
            l1.va[x] = l1.vb[x] + t
        return c

    loop(0, 8, up1, 4)
    l1.sweep(l1.s, l1.va, l1.vb, 6, EX[1] - 6, 6)
    l1.sweep(l1.s, l1.vb, l1.va, 7, EX[1] - 7, 5)

    received(V0)
    all_of(V0).wait_send()
    row = lax.broadcasted_iota(jnp.int32, (EY[0], LANES), 0)
    mine0 = jnp.where((row >= HY[0]) & (row < HY[0] + BY[0]), 1.0, 0.0).astype(f32)

    def up0(i, c):
        t = l1.va[i + 7, pl.ds(8, 32), :]
        rep[i, pl.ds(4, 32, stride=2), :] = t
        rep[i, pl.ds(5, 32, stride=2), :] = t
        t = rep[i, pl.ds(16, EY[0]), :]
        for e in range(2):
            x = 2 * i + 2 + e
            own = mine0 * jnp.where((x >= HX[0]) & (x < HX[0] + BX[0]), 1.0, 0.0).astype(f32)
            near = jnp.where(l0.inside(x) > 0, vh[x] + t, 0.0)
            l0.va[x] = jnp.where(own > 0, l0.vb[x] + t, near)
        return c

    loop(0, 10, up0, 5)
    l0.sweep(l0.s, l0.va, l0.vb, 3, EX[0] - 3, 9)
    def last(x, carry):
        c, near = l0.pull(l0.vb, x)
        t = KEEP * c + l0.inv[x] * (l0.s[x] + near)
        out[x - HX[0]] = t[HY[0] : HY[0] + BY[0]]
        return carry

    loop(HX[0], HX[0] + BX[0], last, 8)
    for phase in range(V0):
        all_of(phase).wait_send()


def solution(mesh):
    nx, ny = mesh.shape["gx"], mesh.shape["gy"]

    def body(defect, coefficient):
        dma = pltpu.SemaphoreType.DMA
        rows = phase_rows(nx, ny)
        scratch = []
        for l in range(3):
            scratch += [pltpu.VMEM((EX[l], EY[l], LANES), f32)] * 9
        scratch += [
            pltpu.VMEM((12, EY[1], LANES), f32),
            pltpu.VMEM((12, 72, LANES), f32),
            pltpu.VMEM((2, EX[2], EY[2], LANES), f32),
            pltpu.VMEM((EX[0], EY[0], LANES), f32),
            pltpu.VMEM((EX[1] // 2, EY[1], LANES), f32),
            pltpu.VMEM((EX[1] // 2, EY[1], LANES), f32),
            pltpu.VMEM((2, 16, LANES), f32),
            pltpu.VMEM((8 * nx, LANES), f32),
            pltpu.VMEM((8 * nx, LANES), f32),
            pltpu.VMEM((3, 2, nx, LANES), f32),
            pltpu.VMEM((2, nx, LANES), f32),
            pltpu.VMEM((3, nx + 16, LANES), f32),
            pltpu.VMEM((8 * ny, LANES), f32),
            pltpu.VMEM((8 * ny, LANES), f32),
            pltpu.VMEM((8, LANES), f32),
            pltpu.VMEM((2, ny + 16, LANES), f32),
            pltpu.VMEM((max(rows), LANES), f32),
            dma((2,)),
            dma((4,)),
            dma((len(rows),)),
            dma((len(rows),)),
            pltpu.SemaphoreType.REGULAR((4,)),
        ]
        return pl.pallas_call(
            functools.partial(kernel, nx, ny),
            out_shape=jax.ShapeDtypeStruct(defect.shape, f32),
            in_specs=[pl.BlockSpec(memory_space=pltpu.HBM)] * 2,
            out_specs=pl.BlockSpec(memory_space=pltpu.VMEM),
            scratch_shapes=scratch,
            compiler_params=pltpu.CompilerParams(
                collective_id=0, has_side_effects=True, vmem_limit_bytes=54784 << 10
            ),
        )(defect, coefficient)

    placed = P("gx", "gy", None)
    return jax.shard_map(
        body, mesh=mesh, in_specs=(placed, placed), out_specs=placed, check_vma=False
    )
```

```python
import functools

import jax
import jax.numpy as jnp
from jax import lax
from jax.experimental import pallas as pl
from jax.experimental.pallas import tpu as pltpu
from jax.sharding import PartitionSpec as P

MESH = pl.DeviceIdType.MESH
DAMP = 0.7
KEEP = 0.3
COARSE_SWEEPS = 8
LANES = 128
f32 = jnp.float32
U0W, U0S, U0R, U1W, U1S, U1R, U2W = 10, 9, 4, 11, 9, 4, 99

BX, BY = (16, 8, 4), (32, 16, 8)
HX, HY = (4, 8, 4), (4, 16, 8)
EX = tuple(b + 2 * h for b, h in zip(BX, HX))
EY = tuple(b + 2 * h for b, h in zip(BY, HY))

NEAR = [(1, 1), (1, -1), (-1, 1), (-1, -1), (1, 0), (-1, 0), (0, 1), (0, -1)]


def ahead(t, d):
    return pltpu.roll(t, (-d) % LANES, axis=t.ndim - 1)


def rows_ahead(t, d):
    n = t.shape[-2]
    return pltpu.roll(t, (-d) % n, axis=t.ndim - 2)


def planes_ahead(t, d):
    d = d % t.shape[0]
    return jnp.concatenate([t[d:], t[:d]], axis=0) if d else t


def lane_iota(shape):
    return lax.broadcasted_iota(jnp.int32, shape, len(shape) - 1)


def bit(lane, b):
    return (lane & (1 << b)) != 0


def swap(t, b):
    on = bit(lane_iota(t.shape), b)
    return jnp.where(on, ahead(t, -(1 << b)), ahead(t, 1 << b))


def spread(t, b, value):
    on = bit(lane_iota(t.shape), b)
    if value:
        return jnp.where(on, t, ahead(t, 1 << b))
    return jnp.where(on, ahead(t, -(1 << b)), t)


def loop(lo, hi, body, unroll=1, carry=()):
    rounds = (hi - lo) // unroll

    def step(r, c):
        for j in range(unroll):
            c = body(lo + unroll * r + j, c)
        return c

    if rounds > 1:
        carry = lax.fori_loop(0, rounds, step, carry)
    else:
        rounds = 0
    for i in range(lo + unroll * rounds, hi):
        carry = body(i, carry)
    return carry


ENTRY = NEAR + [(2, 0), (-2, 0)]
ROUNDS = (
    ((2, 0), (-2, 0), (0, 1), (0, -1)),
    ((4, 0), (-4, 0), (0, 2), (0, -2)),
    ((0, 4), (0, -4)),
    ((0, 8), (0, -8)),
)

K0, S0, K1, S1, GA, SV, GB, H3, K0Y, S0Y, S1Y, GK, KB, V0 = range(14)


def slabs(ref, halo, block, wide):
    parts = []
    for offset in NEAR:
        spans = []
        for d, h, b, w in zip(offset, halo, block, wide):
            if d == 0:
                spans.append((h, h, b))
            elif d > 0:
                spans.append((h + b - w, h - w, w))
            else:
                spans.append((h, h + b, w))
        (sx, tx, cx), (sy, ty, cy) = spans
        parts.append(
            (
                ref.at[pl.ds(sx, cx), pl.ds(sy, cy), :],
                ref.at[pl.ds(tx, cx), pl.ds(ty, cy), :],
            )
        )
    return parts


def both(low, high):
    return jnp.where(bit(lane_iota(low.shape), 0), high, low)


def apart(t):
    odd = bit(lane_iota(t.shape), 0)
    return jnp.where(odd, ahead(t, -1), t), jnp.where(odd, t, ahead(t, 1))


def phase_rows(nx, ny):
    def beside(level, wy):
        return BX[level] // (2 if level == 1 else 1) * 2 * wy

    def rim(level, wx, wy):
        bx, by = BX[level] // (2 if level == 1 else 1), BY[level]
        return (bx + 2 * wx) * (by + 2 * wy) - bx * by

    def ends(level, wx, wy):
        return rim(level, wx, wy) - beside(level, wy)

    return (
        ends(0, 3, 3),
        ends(0, 2, 2),
        rim(1, 4, 16),
        ends(1, 3, 14),
        2 * (nx - 1),
        2 * rim(2, 4, 4),
        2 * (ny - 1),
        4 * nx,
        beside(0, 3),
        beside(0, 2),
        beside(1, 14),
        3 * (nx - 1),
        2 * (ny - 1),
        rim(0, 2, 2),
    )


class Block:
    def __init__(self, level, gx, gy, nx, ny, refs):
        self.level = level
        self.factor = 0.25**level
        self.zs = 1 << level
        self.bx, self.by, self.hx, self.hy = BX[level], BY[level], HX[level], HY[level]
        self.ex, self.ey = EX[level], EY[level]
        self.gx, self.gy, self.nx, self.ny = gx, gy, nx, ny
        self.k, self.s, self.va, self.vb, self.wx, self.wy, self.wz, self.inv, self.dg = refs
        shape = (self.ey, LANES)
        self.lane = lane_iota(shape)
        y = gy * self.by - self.hy + lax.broadcasted_iota(jnp.int32, shape, 0)
        self.row_in = jnp.where((y >= 0) & (y < ny * self.by), 1.0, 0.0).astype(f32)

    def inside(self, x):
        gx = self.gx * self.bx - self.hx + x
        return self.row_in * jnp.where((gx >= 0) & (gx < self.nx * self.bx), 1.0, 0.0).astype(f32)

    def weights(self, lo, hi, unroll=1):
        half = 0.5 * self.factor
        last = self.lane >= LANES - self.zs
        first = self.lane < self.zs

        def step(x, carry):
            kc, fxm = carry
            m = self.inside(x)
            kn = self.k[x + 1] * self.inside(x + 1)
            fxp = half * (kc + kn)
            fyp = half * (kc + rows_ahead(kc, 1))
            fzp = half * (kc + jnp.where(last, 0.0, ahead(kc, self.zs)))
            wz = jnp.where(last, 0.0, fzp)
            fzm = jnp.where(first, half * kc, ahead(wz, -self.zs))
            diag = ((fxm + fxp) + (rows_ahead(fyp, -1) + fyp)) + (fzp + fzm)
            self.wx[x] = fxp
            self.wy[x] = fyp
            self.wz[x] = wz
            self.dg[x] = diag
            self.inv[x] = jnp.where(m > 0, DAMP / diag, 0.0)
            return kn, fxp

        k0 = self.k[lo - 1] * self.inside(lo - 1)
        k1 = self.k[lo] * self.inside(lo)
        self.wx[lo - 1] = half * (k0 + k1)
        loop(lo, hi, step, unroll, (k1, half * (k0 + k1)))

    def first(self, src, dst, lo, hi, unroll=1):
        def step(x, c):
            dst[x] = self.inv[x] * src[x]
            return c

        loop(lo, hi, step, unroll)

    def pull(self, v, x):
        c = v[x]
        wy, wz = self.wy[x], self.wz[x]
        t = self.wx[x] * v[x + 1] + self.wx[x - 1] * v[x - 1]
        u = wy * rows_ahead(c, 1) + rows_ahead(wy * c, -1)
        w = wz * ahead(c, self.zs) + ahead(wz * c, -self.zs)
        return c, (t + u) + w

    def sweep(self, s, src, dst, lo, hi, unroll=1, shift=0):
        def step(x, carry):
            c, near = self.pull(src, x)
            dst[x - shift] = KEEP * c + self.inv[x] * (s[x] + near)
            return carry

        loop(lo, hi, step, unroll)

    def residual(self, s, v, x):
        c, near = self.pull(v, x)
        return (s[x] - self.dg[x] * c) + near

    def restrict(self, plane, tmp, lo, pairs, row, count, put, unroll=1):
        lane = lane_iota((count, LANES))

        def step(i, c):
            x = lo + 2 * i
            t = plane(x) + plane(x + 1)
            tmp[i, pl.ds(0, t.shape[0]), :] = t
            t = tmp[i, pl.ds(row, count, stride=2), :] + tmp[i, pl.ds(row + 1, count, stride=2), :]
            put(i, 0.125 * (t + swap(t, self.level)))
            return c

        loop(0, pairs, step, unroll)


class Whole:
    def __init__(self, factor, k, near, masks, inside=None):
        half = 0.5 * factor
        self.near = near
        faces, parts = [], []
        for n, mask in zip(near(k), masks):
            face = half * (k + n)
            faces.append(jnp.where(mask, face, 0.0))
            parts.append(jnp.where(mask, face, half * k))
        diag = (parts[0] + parts[1]) + (parts[2] + parts[3]) + (parts[4] + parts[5])
        inv = DAMP / diag
        self.inv = inv if inside is None else jnp.where(inside, inv, 0.0)
        self.w = [face * self.inv for face in faces]
        self.back = diag * (1.0 / DAMP)

    def pull(self, v):
        t = [w * n for w, n in zip(self.w, self.near(v))]
        return (t[0] + t[1]) + (t[2] + t[3]) + (t[4] + t[5])

    def sweep(self, q, v):
        return (KEEP * v + q) + self.pull(v)

    def residual(self, q, v):
        return ((q - DAMP * v) + self.pull(v)) * self.back


def kernel(nx, ny, *refs):
    s_in, k_in, out = refs[:3]
    level_refs = [refs[3 + 9 * l : 12 + 9 * l] for l in range(3)]
    (
        tmp, rep, sv2, vh, k1p, s1p, pack, acc, acck, halo3, v3s, v3u, bcs, bck, own4, v4s, ruler,
        local_sem, out_sem, ssem, rsem, known,
    ) = refs[30:]
    gx, gy = lax.axis_index("gx"), lax.axis_index("gy")
    ROWS = phase_rows(nx, ny)

    def there(dx, dy):
        return (lax.rem(gx + dx + nx, nx), lax.rem(gy + dy + ny, ny))

    L = [Block(l, gx, gy, nx, ny, level_refs[l]) for l in range(3)]
    l0, l1, l2 = L
    own0 = (pl.ds(HX[0], BX[0]), pl.ds(HY[0], BY[0]))
    loads = [
        pltpu.make_async_copy(k_in, l0.k.at[own0[0], own0[1], :], local_sem.at[0]),
        pltpu.make_async_copy(s_in, l0.s.at[own0[0], own0[1], :], local_sem.at[1]),
    ]

    column = [(i, 0) for i in range(1, nx)]
    line = [(0, j) for j in range(1, ny)]
    line.sort(key=lambda o: -sum(min(c % 4, -c % 4) for c in (o[1] // 2, o[1] // 8)))
    column.sort(key=lambda o: -min(o[0], nx - o[0]))
    barrier = pltpu.get_barrier_semaphore()
    for dx, dy in ENTRY:
        pl.semaphore_signal(barrier, inc=1, device_id=there(dx, dy), device_id_type=MESH)
    for c in loads:
        c.start()
    v3u[...] = jnp.zeros_like(v3u)
    for c in loads:
        c.wait()

    half1 = (HX[1] // 2, HY[1]), (BX[1] // 2, BY[1])

    def put_k1(i, t):
        l1.k[HX[1] + i, pl.ds(HY[1], BY[1]), :] = t

    def pair_up(src, dst):
        for i in range(BX[1] // 2):
            x = HX[1] + 2 * i
            low, high = (src[x + j, pl.ds(HY[1], BY[1]), :] for j in range(2))
            dst[HX[1] // 2 + i, pl.ds(HY[1], BY[1]), :] = both(low, high)

    def split(src, dst, lo, hi, unroll, start=False):
        def step(i, c):
            for x, t in zip((2 * i, 2 * i + 1), apart(src[i])):
                dst[x] = t
                if start:
                    l1.va[x] = l1.inv[x] * t
            return c

        loop(lo, hi, step, unroll)

    l0.restrict(lambda x: l0.k[x, own0[1], :], tmp, HX[0], BX[1], 0, BY[1], put_k1, U0R)
    pair_up(l1.k, k1p)

    pl.semaphore_wait(barrier, len(ENTRY))

    def remote(src, dst, phase, dx, dy):
        c = pltpu.make_async_remote_copy(
            src, dst, ssem.at[phase], rsem.at[phase], device_id=there(dx, dy), device_id_type=MESH
        )
        c.start()

    def tell(step):
        for dx, dy in ROUNDS[step]:
            pl.semaphore_signal(known.at[step], inc=1, device_id=there(dx, dy), device_id_type=MESH)

    def told(step):
        pl.semaphore_wait(known.at[step], len(ROUNDS[step]))

    def all_of(phase):
        part = ruler.at[pl.ds(0, ROWS[phase]), :]
        return pltpu.make_async_remote_copy(
            part, part, ssem.at[phase], rsem.at[phase], device_id=there(1, 0), device_id_type=MESH
        )

    def received(phase):
        all_of(phase).wait_recv()

    def send(parts, phase, phase_y=None):
        for (dx, dy), (src, dst) in zip(NEAR, parts):
            remote(src, dst, phase if dx or phase_y is None else phase_y, dx, dy)

    tell(0)
    send(slabs(l0.k, (HX[0], HY[0]), (BX[0], BY[0]), (3, 3)), K0, K0Y)
    send(slabs(l0.s, (HX[0], HY[0]), (BX[0], BY[0]), (2, 2)), S0, S0Y)

    send(slabs(k1p, half1[0], half1[1], (4, 16)), K1)
    told(0)
    tell(1)

    def residual0(lo, pairs):
        def put(i, t):
            l1.s[HX[1] + (lo - HX[0]) // 2 + i, pl.ds(HY[1], BY[1]), :] = t

        l0.restrict(lambda x: l0.residual(l0.s, l0.vb, x), tmp, lo, pairs, HY[0], BY[1], put, 4)

    received(K0Y)
    l0.weights(5, 19, 7)
    received(S0Y)
    l0.first(l0.s, l0.va, 5, 19, 7)
    l0.sweep(l0.s, l0.va, l0.vb, 6, 18, 6)
    residual0(8, 4)
    received(K0)
    l0.weights(2, 5, 3)
    l0.weights(19, 22, 3)
    received(S0)
    l0.first(l0.s, l0.va, 2, 5, 3)
    l0.first(l0.s, l0.va, 19, 22, 3)
    l0.sweep(l0.s, l0.va, l0.vb, 3, 6, 3)
    l0.sweep(l0.s, l0.va, l0.vb, 18, 21, 3)
    residual0(4, 2)
    residual0(16, 2)
    pair_up(l1.s, s1p)
    send(slabs(s1p, half1[0], half1[1], (3, 14)), S1, S1Y)
    told(1)
    tell(2)
    received(K1)
    split(k1p, l1.k, 0, EX[1] // 2, 6)

    def put_k2(i, t):
        l2.k[i] = t

    l1.restrict(lambda x: l1.k[x], tmp, 0, EX[2], 0, EY[2], put_k2, 6)
    l1.weights(1, EX[1] - 1, U1W)
    l2.weights(1, EX[2] - 1, U2W)

    def packed(count, base, blocks):
        sub = lax.broadcasted_iota(jnp.int32, (count, LANES), 0)
        lane = lane_iota((count, LANES))
        low, high = (pack[i, pl.ds(0, count), :] for i in range(2))
        y = (sub + base) & 3
        t = jnp.where(lane & 7 == y, low, jnp.where(lane & 7 == 4 + y, high, 0.0))
        on = (lane & 3) == y
        return [jnp.sum(jnp.where(on & block(sub), t, 0.0), axis=0, keepdims=True) for block in blocks]

    def put_pack(i, t):
        pack[i, pl.ds(0, t.shape[0]), :] = t

    l2.restrict(lambda x: l2.k[x], tmp, HX[2], 2, 0, 12, put_pack, unroll=99)
    mine = pl.multiple_of(8 * gx, 8)
    blocks = [lambda r, g=g: (r >> 2) == g for g in range(3)]
    acck[pl.ds(mine, 3), :] = jnp.concatenate(packed(16, 0, blocks), axis=0)
    for dx, dy in column:
        remote(acck.at[pl.ds(mine, 3), :], acck.at[pl.ds(mine, 3), :], GK, dx, dy)

    def residual1(lo, pairs):
        def put(i, t):
            l2.s[lo // 2 + i] = t

        l1.restrict(lambda x: l1.residual(l1.s, l1.vb, x), tmp, lo, pairs, 0, EY[2], put, 3)

    received(S1Y)
    split(s1p, l1.s, 4, 8, 4, start=True)
    l1.sweep(l1.s, l1.va, l1.vb, 9, 15, 6)
    residual1(10, 2)
    received(S1)
    split(s1p, l1.s, 1, 4, 3, start=True)
    split(s1p, l1.s, 8, 11, 3, start=True)
    l1.sweep(l1.s, l1.va, l1.vb, 3, 9, 6)
    l1.sweep(l1.s, l1.va, l1.vb, 15, 21, 6)
    residual1(4, 3)
    residual1(14, 3)

    l2.first(l2.s, l2.va, 2, EX[2] - 2, unroll=99)
    l2.sweep(l2.s, l2.va, l2.vb, 3, EX[2] - 3, unroll=99)
    l2.restrict(lambda x: l2.residual(l2.s, l2.vb, x), tmp, HX[2], 2, HY[2] - 4, 8, put_pack, unroll=99)
    blocks = [lambda r: (r >= 2) & (r < 6), lambda r: (r < 2) | (r >= 6)]
    acc[pl.ds(mine, 2), :] = jnp.concatenate(packed(8, 2, blocks), axis=0)

    for dx, dy in column:
        remote(acc.at[pl.ds(mine, 2), :], acc.at[pl.ds(mine, 2), :], GA, dx, dy)

    told(2)
    tell(3)
    received(GK)

    shape = (3, nx, LANES)
    lane = lane_iota(shape)
    px = lax.broadcasted_iota(jnp.int32, shape, 1)
    py = gy - 1 + lax.broadcasted_iota(jnp.int32, shape, 0)
    b2, yl, z3 = bit(lane, 2), lane & 3, lane >> 3

    def near3(v):
        up, down = ahead(v, 4), ahead(v, -4)
        return (
            jnp.where(b2, rows_ahead(down, 1), up),
            jnp.where(b2, down, rows_ahead(up, -1)),
            jnp.where(yl == 3, planes_ahead(ahead(v, -3), 1), ahead(v, 1)),
            jnp.where(yl == 0, planes_ahead(ahead(v, 3), -1), ahead(v, -1)),
            ahead(v, 8),
            ahead(v, -8),
        )

    x3, y3 = 2 * px + jnp.where(b2, 1, 0), 4 * py + yl
    in3 = (py >= 0) & (py < ny)
    k3 = jnp.stack([acck[pl.ds(q, nx, stride=8), :] for q in range(3)])
    w3 = Whole(
        0.25**3,
        jnp.where(in3, k3, 0.0),
        near3,
        (x3 < 2 * nx - 1, x3 > 0, y3 < 4 * ny - 1, y3 > 0, z3 < 15, z3 > 0),
        in3,
    )
    shape = (nx, LANES)
    lane, sub = lane_iota(shape), lax.broadcasted_iota(jnp.int32, shape, 0)
    place = ((lane >> 1) & 6) + (lane & 1) == (sub >> 1)
    odd = (sub & 1) != 0

    def coarse4(t):
        t = t + swap(t, 2)
        t = t + swap(t, 0)
        t = 0.125 * (t + swap(t, 3))
        t = jnp.where(place, t, 0.0)
        return [jnp.sum(jnp.where(odd == h, t, 0.0), axis=0, keepdims=True) for h in (False, True)]

    def share4(rows, first, bcc, phase):
        own4[pl.ds(first, 2), :] = rows
        there4 = pl.ds(pl.multiple_of(8 * gy, 8), 2)
        bcc[there4, :] = rows
        for dx, dy in line:
            remote(own4.at[pl.ds(first, 2), :], bcc.at[there4, :], phase, dx, dy)

    told(3)
    share4(jnp.concatenate(coarse4(k3[1]), axis=0), 2, bck, KB)

    received(GA)
    own3, side3 = (acc[pl.ds(q, nx, stride=8), :] for q in range(2))
    src3 = jnp.stack([side3, own3, side3])
    q3 = w3.inv * src3
    v = w3.sweep(q3, q3)
    v3s[0], v3s[1] = v[1], own3
    r3 = w3.residual(q3, v)[1]

    share4(jnp.concatenate(coarse4(r3), axis=0), 0, bcs, GB)
    for dy in (1, -1):
        remote(v3s, halo3.at[1 - dy], H3, 0, dy)
    for (dx, dy), (src, _), (_, dst) in zip(NEAR, slabs(l0.vb, (HX[0], HY[0]), (BX[0], BY[0]), (2, 2)), slabs(vh, (HX[0], HY[0]), (BX[0], BY[0]), (2, 2))):
        remote(src, dst, V0, dx, dy)

    own2 = (pl.ds(HX[2], BX[2]), pl.ds(HY[2], BY[2]))
    sv2[0, own2[0], own2[1], :] = l2.s[own2[0], own2[1], :]
    sv2[1, own2[0], own2[1], :] = l2.vb[own2[0], own2[1], :]
    for q in range(2):
        send(slabs(sv2.at[q], (HX[2], HY[2]), (BX[2], BY[2]), (4, 4)), SV)

    received(KB)

    k4 = jnp.stack([bck[pl.ds(h, ny, stride=8), :] for h in range(2)])
    shape = (2, ny, LANES)
    lane = lane_iota(shape)
    plane = lax.broadcasted_iota(jnp.int32, shape, 0)
    b1 = bit(lane, 1)
    y4, z4 = 2 * lax.broadcasted_iota(jnp.int32, shape, 1) + jnp.where(b1, 1, 0), lane >> 4
    lane2, row = lane_iota((ny, LANES)), lax.broadcasted_iota(jnp.int32, (ny, LANES), 0)
    c0 = bit(lane2, 0)

    def plus(t):
        return jnp.where(c0, ahead(t, 3), ahead(t, 1))

    def minus(t):
        return jnp.where(c0, ahead(t, -1), ahead(t, -3))

    def near4(v):
        up, down = ahead(v, 2), ahead(v, -2)
        return (
            jnp.stack([v[1], plus(v[0])]),
            jnp.stack([minus(v[1]), v[0]]),
            jnp.where(b1, rows_ahead(down, 1), up),
            jnp.where(b1, down, rows_ahead(up, -1)),
            ahead(v, 16),
            ahead(v, -16),
        )

    w4 = Whole(
        0.25**4,
        k4,
        near4,
        (
            (lane & 13 < 13) | (plane < 1),
            (lane & 13 > 0) | (plane > 0),
            y4 < 2 * ny - 1,
            y4 > 0,
            z4 < 7,
            z4 > 0,
        ),
    )

    def coarse5(t):
        t = t[0] + t[1]
        t = t + swap(t, 1)
        return 0.125 * (t + swap(t, 4))

    def near5(v):
        return plus(v), minus(v), rows_ahead(v, 1), rows_ahead(v, -1), ahead(v, 32), ahead(v, -32)

    x5, z5 = lane2 & 13, lane2 >> 5
    k5 = coarse5(k4)
    w5 = Whole(0.25**5, k5, near5, (x5 < 13, x5 > 0, row < ny - 1, row > 0, z5 < 3, z5 > 0))

    def coarse6(t):
        t = t + swap(t, 0)
        t = t + swap(t, 5)
        return 0.125 * (t + jnp.where((row & 1) != 0, rows_ahead(t, -1), rows_ahead(t, 1)))

    def near6(v):
        turned = ahead(v, 64)
        return ahead(v, 4), ahead(v, -4), rows_ahead(v, 2), rows_ahead(v, -2), turned, turned

    x6, z6 = (lane2 >> 2) & 3, lane2 >> 6
    w6 = Whole(0.25**6, coarse6(k5), near6, (x6 < 3, x6 > 0, row < ny - 2, row > 1, z6 < 1, z6 > 0))

    received(GB)
    s4 = jnp.stack([bcs[pl.ds(h, ny, stride=8), :] for h in range(2)])
    q4 = w4.inv * s4
    v4 = w4.sweep(q4, q4)
    q5 = w5.inv * coarse5(w4.residual(q4, v4))
    v5 = w5.sweep(q5, q5)
    q6 = w6.inv * coarse6(w5.residual(q5, v5))
    v6 = q6
    for _ in range(COARSE_SWEEPS - 1):
        v6 = w6.sweep(q6, v6)
    v5 = v5 + v6
    v5 = w5.sweep(q5, v5)
    v5 = w5.sweep(q5, v5)
    v4 = v4 + v5[None]
    v4 = w4.sweep(q4, v4)
    v4 = w4.sweep(q4, v4)
    v4s[:, pl.ds(8, ny), :] = v4

    received(H3)
    below = []
    for g in range(3):
        t = [jnp.broadcast_to(v4s[h, pl.ds(7 + gy + g, 1), :], (nx, LANES)) for h in range(2)]
        t = jnp.where(place, jnp.where(odd, t[1], t[0]), 0.0)
        for b in (0, 2, 3):
            t = t + swap(t, b)
        below.append(t)
    q3 = w3.inv * jnp.stack([halo3[0, 1], own3, halo3[2, 1]])
    v = jnp.stack([halo3[0, 0], v3s[0], halo3[2, 0]]) + jnp.stack(below)
    v = jnp.where(in3, v, 0.0)
    v = w3.sweep(q3, v)
    v = w3.sweep(q3, v)
    v3u[:, pl.ds(8, nx), :] = v

    received(SV)
    shape = (8, LANES)
    lane, sub = lane_iota(shape), lax.broadcasted_iota(jnp.int32, shape, 0)
    for d in range(3):
        rows = [jnp.broadcast_to(v3u[g, pl.ds(7 + gx + d, 1), :], shape) for g in range(3)]
        rows = jnp.where(sub < 2, rows[0], jnp.where(sub < 6, rows[1], rows[2]))
        for xl in range(2):
            t = jnp.where((lane & 7) == 4 * xl + ((sub + 2) & 3), rows, 0.0)
            for b in range(3):
                t = t + swap(t, b)
            n = 2 * d + xl
            rep[n, pl.ds(4, 8, stride=2), :] = t
            rep[n, pl.ds(5, 8, stride=2), :] = t
            t = rep[n, pl.ds(0, EY[2]), :]
            for e in range(2):
                x = 2 * n + e
                l2.va[x] = jnp.where(l2.inside(x) > 0, sv2[1, x] + t, 0.0)
    l2.sweep(sv2.at[0], l2.va, l2.vb, 1, EX[2] - 1, unroll=99)
    l2.sweep(sv2.at[0], l2.vb, l2.va, 2, EX[2] - 2, unroll=99)

    def up1(i, c):
        t = l2.va[i + 2]
        rep[i, pl.ds(0, EY[2], stride=2), :] = t
        rep[i, pl.ds(1, EY[2], stride=2), :] = t
        t = rep[i, pl.ds(0, EY[1]), :]
        for e in range(2):
            x = 2 * i + 4 + e
            l1.va[x] = l1.vb[x] + t
        return c

    loop(0, 8, up1, 4)
    l1.sweep(l1.s, l1.va, l1.vb, 6, EX[1] - 6, 6)
    l1.sweep(l1.s, l1.vb, l1.va, 7, EX[1] - 7, 5)

    received(V0)
    all_of(V0).wait_send()
    row = lax.broadcasted_iota(jnp.int32, (EY[0], LANES), 0)
    mine0 = jnp.where((row >= HY[0]) & (row < HY[0] + BY[0]), 1.0, 0.0).astype(f32)

    def up0(i, c):
        t = l1.va[i + 7, pl.ds(8, 32), :]
        rep[i, pl.ds(4, 32, stride=2), :] = t
        rep[i, pl.ds(5, 32, stride=2), :] = t
        t = rep[i, pl.ds(16, EY[0]), :]
        for e in range(2):
            x = 2 * i + 2 + e
            own = mine0 * jnp.where((x >= HX[0]) & (x < HX[0] + BX[0]), 1.0, 0.0).astype(f32)
            near = jnp.where(l0.inside(x) > 0, vh[x] + t, 0.0)
            l0.va[x] = jnp.where(own > 0, l0.vb[x] + t, near)
        return c

    loop(0, 10, up0, 5)
    l0.sweep(l0.s, l0.va, l0.vb, 3, EX[0] - 3, 9)
    def last(x, carry):
        c, near = l0.pull(l0.vb, x)
        t = KEEP * c + l0.inv[x] * (l0.s[x] + near)
        out[x - HX[0]] = t[HY[0] : HY[0] + BY[0]]
        return carry

    loop(HX[0], HX[0] + BX[0], last, 8)
    for phase in range(V0):
        all_of(phase).wait_send()


def solution(mesh):
    nx, ny = mesh.shape["gx"], mesh.shape["gy"]

    def body(defect, coefficient):
        dma = pltpu.SemaphoreType.DMA
        rows = phase_rows(nx, ny)
        scratch = []
        for l in range(3):
            scratch += [pltpu.VMEM((EX[l], EY[l], LANES), f32)] * 9
        scratch += [
            pltpu.VMEM((12, EY[1] + 8, LANES), f32),
            pltpu.VMEM((12, 72, LANES), f32),
            pltpu.VMEM((2, EX[2], EY[2], LANES), f32),
            pltpu.VMEM((EX[0], EY[0], LANES), f32),
            pltpu.VMEM((EX[1] // 2, EY[1], LANES), f32),
            pltpu.VMEM((EX[1] // 2, EY[1], LANES), f32),
            pltpu.VMEM((2, 16, LANES), f32),
            pltpu.VMEM((8 * nx + 8, LANES), f32),
            pltpu.VMEM((8 * nx + 8, LANES), f32),
            pltpu.VMEM((3, 2, nx, LANES), f32),
            pltpu.VMEM((2, nx, LANES), f32),
            pltpu.VMEM((3, nx + 24, LANES), f32),
            pltpu.VMEM((8 * ny + 8, LANES), f32),
            pltpu.VMEM((8 * ny + 8, LANES), f32),
            pltpu.VMEM((16, LANES), f32),
            pltpu.VMEM((2, ny + 24, LANES), f32),
            pltpu.VMEM((max(rows), LANES), f32),
            dma((2,)),
            dma((4,)),
            dma((len(rows),)),
            dma((len(rows),)),
            pltpu.SemaphoreType.REGULAR((4,)),
        ]
        return pl.pallas_call(
            functools.partial(kernel, nx, ny),
            out_shape=jax.ShapeDtypeStruct(defect.shape, f32),
            in_specs=[pl.BlockSpec(memory_space=pltpu.HBM)] * 2,
            out_specs=pl.BlockSpec(memory_space=pltpu.VMEM),
            scratch_shapes=scratch,
            compiler_params=pltpu.CompilerParams(
                collective_id=0, has_side_effects=True, vmem_limit_bytes=54784 << 10
            ),
        )(defect, coefficient)

    placed = P("gx", "gy", None)
    return jax.shard_map(
        body, mesh=mesh, in_specs=(placed, placed), out_specs=placed, check_vma=False
    )
```
